256 devices in a mesh: dp: 8 (over y, core), space: 32 (over z, x).
Axes of the slice: x: 4, y: 4, z: 8, core: 2. Of those that a mesh axis runs over, the one named last changes fastest.
Arguments:
- features: bfloat16 [8, 32, 512, 256], P('dp', 'space'), may hold values from -6 to 6
- occupancy: int32 [8, 32, 512], P('dp', 'space'), may hold values 0 or 1
- nbr_slots: int32 [8, 32, 26], P('dp', 'space'), may hold values from 0 to 6, as said below
- send_mask: int32 [8, 32, 6], P('dp', 'space'), may hold values from 0 to 1, as said below
- cotangent: bfloat16 [8, 32, 512, 256], P('dp', 'space'), may hold values from -0.06591797 to 0.06591797
- weight_one: bfloat16 [27, 256, 256], replicated, may hold values from -0.078125 to 0.078125
- weight_two: bfloat16 [27, 256, 256], replicated, may hold values from -0.078125 to 0.078125
Outputs:
- grad_one: float32 [256, 27, 256], P('space')
- grad_two: float32 [256, 27, 256], P('space')
The draws below stay inside these ranges and needn't reach their ends.
Inputs may be any that keep to these rules, and one draw needn't show every extreme that they name: Bricks of a scene lie in curve order: every brick adjacent to brick i (the 26 brick offsets) is brick i + d with 1 <= |d| <= 3, and nbr_slots names exactly these, 6 elsewhere. send_mask[i, s] is 1 exactly where brick i + d_s has brick i among its neighbours.
All inputs are finite; a program needn't handle non-finite values. No bound on the sum of `occupancy` on one device may be relied on, other than what follows from the above.
Results may differ from the reference program's by a relative error of at most 0.0042.
Values may be sent and summed in bfloat16 or wider, within the bound.
A program may use at most 128 MiB of HBM per device.

```python
import jax
import jax.numpy as jnp
import numpy as np
from jax import lax

C = 256
E = 8
VOX = 512
SCENES = 8
NB = 32


MOVE_TABLE = np.array([[1, 0, 0], [0, 1, 0], [0, -1, 0], [0, 0, 1], [0, 0, -1]], np.int32)


NEAR_OFFSETS = np.array([[a, b, c] for a in (-1, 0, 1) for b in (-1, 0, 1) for c in (-1, 0, 1) if (a, b, c) != (0, 0, 0)], np.int32)


DISTANCES = (-3, -2, -1, 1, 2, 3)


def walk_coords(key):
    kinds = jax.random.randint(key, (SCENES, NB), 0, 5)
    steps_index = jnp.arange(NB)
    kinds = jnp.where(steps_index[None, :] % 2 == 0, 0, kinds)
    moves = jnp.asarray(MOVE_TABLE)[kinds] * (steps_index > 0).astype(jnp.int32)[None, :, None]
    return jnp.cumsum(moves, axis=1).astype(jnp.int32)


def slot_table(coords):
    padded = jnp.pad(coords, ((0, 0), (3, 3), (0, 0)), constant_values=100000)
    offsets = jnp.asarray(NEAR_OFFSETS)
    result = jnp.full((SCENES, NB, 26), 6, jnp.int32)
    for position, dist in enumerate(DISTANCES):
        other = padded[:, 3 + dist:3 + dist + NB]
        diff = other - coords
        match = jnp.all(diff[:, :, None, :] == offsets[None, None], axis=-1)
        result = jnp.where(match, position, result)
    return result


def draw_nbr_slots(key, part):
    coords = walk_coords(key)
    key = jax.random.fold_in(key, 11)
    return slot_table(coords)


def draw_send_mask(key, part):
    coords = walk_coords(key)
    key = jax.random.fold_in(key, 12)
    table = slot_table(coords)
    return jnp.stack([jnp.any(table == position, axis=-1) for position in range(6)], axis=-1).astype(jnp.int32)


def set_ends(drawn, rng, least, largest):
    longest = drawn.shape.index(max(drawn.shape))
    spots = []
    for shift in (0, 1):
        where = [jax.random.randint(jax.random.fold_in(rng, axis), (), 0, length) for axis, length in enumerate(drawn.shape)]
        where[longest] = (where[longest] + shift) % drawn.shape[longest]
        spots.append(tuple(where))
    return drawn.at[spots[0]].set(least).at[spots[1]].set(largest)


def levels(own_key, extent, split, smallest, top_value):
    def one(dim, blocks):
        draws = jax.random.uniform(jax.random.fold_in(jax.random.fold_in(own_key, 6), dim), (blocks,), jnp.float32, smallest / len(split), top_value / len(split))
        return jnp.repeat(jnp.exp(draws), extent[dim] // blocks).reshape((-1,) + (1,) * (len(extent) - dim - 1))

    level = one(*split[0])
    for cut in split[1:]:
        level = level * one(*cut)
    return level


def noise(stream_key, extent, width, most, split=(), kind=jnp.bfloat16):
    entries = jax.random.normal(stream_key, extent, jnp.float32) * width
    if len(split) > 0:
        entries = levels(stream_key, extent, split, -0.22, 0.18) * entries
    return jnp.clip(entries, min=-most, max=most).astype(kind)


def setup_inputs(seed: int = 0) -> dict:
    arg_keys = jax.random.split(jax.random.key(seed), 8)
    return {
        "features": noise(arg_keys[0], (SCENES, NB, VOX, C), 1.0, 6.0, ((0, 8), (1, 32))),
        "occupancy": set_ends((jax.random.randint(arg_keys[1], (SCENES, NB, VOX), 0, 2) < 1).astype(jnp.int32), jax.random.fold_in(arg_keys[1], 1), 0, 1),
        "nbr_slots": draw_nbr_slots(jax.random.fold_in(arg_keys[7], 71), 0),
        "send_mask": draw_send_mask(jax.random.fold_in(arg_keys[7], 71), 0),
        "cotangent": noise(arg_keys[4], (SCENES, NB, VOX, C), (4.0 / (SCENES * NB * VOX) ** 0.5), 0.06591797, ((0, 8), (1, 32))),
        "weight_one": noise(arg_keys[5], (27, C, C), (27 * C) ** -0.5, 0.078125),
        "weight_two": noise(arg_keys[6], (27, C, C), (27 * C) ** -0.5, 0.078125),
    }


OFFSETS = [(a, b, c) for a in (-1, 0, 1) for b in (-1, 0, 1) for c in (-1, 0, 1)]
DISTANCES = (-3, -2, -1, 1, 2, 3)


def pick_range(shift, brick_edge):
    if shift == -1:
        return slice(brick_edge - 1, brick_edge)
    if shift == 0:
        return slice(0, brick_edge)
    return slice(0, 1)


def assemble(own_brick, table, slot_row, brick_edge):
    planes = []
    for a in (-1, 0, 1):
        rows_out = []
        for b in (-1, 0, 1):
            pieces = []
            for c in (-1, 0, 1):
                number = (a + 1) * 9 + (b + 1) * 3 + (c + 1)
                if number == 13:
                    block = own_brick
                else:
                    index = number if number < 13 else number - 1
                    block = lax.dynamic_index_in_dim(table, slot_row[index], 0, keepdims=False)
                pieces.append(block[pick_range(a, brick_edge), pick_range(b, brick_edge), pick_range(c, brick_edge)])
            rows_out.append(jnp.concatenate(pieces, axis=2))
        planes.append(jnp.concatenate(rows_out, axis=1))
    return jnp.concatenate(planes, axis=0)


def windows(padded, brick_edge):
    chans = padded.shape[-1]
    return jnp.stack([padded[1 + a:1 + a + brick_edge, 1 + b:1 + b + brick_edge, 1 + c:1 + c + brick_edge].reshape(brick_edge ** 3, chans) for (a, b, c) in OFFSETS])


def conv_forward(padded, weight):
    wins = windows(padded, E)
    return jnp.einsum('kvc,kcd->vd', wins.astype(jnp.float32), weight.astype(jnp.float32))


def conv_transpose(padded, weight):
    wins = windows(padded, E)[::-1]
    return jnp.einsum('kvd,kcd->vc', wins.astype(jnp.float32), weight.astype(jnp.float32))


def weight_terms(padded, grad):
    wins = windows(padded, E)
    return jnp.einsum('kvc,vd->ckd', wins.astype(jnp.float32), grad.astype(jnp.float32))


def halo_blocks(field, slot_rows, send_rows):
    bricks = field.reshape(NB, E, E, E, C)
    padded = jnp.pad(bricks, ((3, 3), (0, 0), (0, 0), (0, 0), (0, 0)))
    send_pad = jnp.pad(send_rows, ((3, 3), (0, 0))).astype(field.dtype)
    parts = []
    for position, dist in enumerate(DISTANCES):
        factor = send_pad[3 + dist:3 + dist + NB, 5 - position]
        parts.append(padded[3 + dist:3 + dist + NB] * factor[:, None, None, None, None])
    parts.append(jnp.zeros_like(bricks))
    table = jnp.stack(parts, axis=1)
    return jax.vmap(lambda own, tab, row: assemble(own, tab, row, E))(bricks, table, slot_rows)


def silu_slope(value):
    sig = jax.nn.sigmoid(value)
    return sig * (1.0 + value * (1.0 - sig))


def one_scene(features, occupancy, slot_rows, send_rows, cotangent, weight_one, weight_two):
    occupied = occupancy.astype(jnp.float32)[:, :, None]
    masked = features * occupancy.astype(jnp.bfloat16)[:, :, None]
    padded_in = halo_blocks(masked, slot_rows, send_rows)
    pre_one = lax.map(lambda p: conv_forward(p, weight_one), padded_in) * occupied
    hidden = (pre_one * jax.nn.sigmoid(pre_one)).astype(jnp.bfloat16)
    padded_hidden = halo_blocks(hidden, slot_rows, send_rows)
    pre_two = lax.map(lambda p: conv_forward(p, weight_two), padded_hidden) * occupied + masked.astype(jnp.float32)
    grad_out = (cotangent.astype(jnp.float32) * silu_slope(pre_two) * occupied).astype(jnp.bfloat16)
    padded_grad = halo_blocks(grad_out, slot_rows, send_rows)
    grad_hidden = lax.map(lambda p: conv_transpose(p, weight_two), padded_grad)
    grad_pre = (grad_hidden * silu_slope(pre_one) * occupied).astype(jnp.bfloat16)
    zeros = jnp.zeros((C, 27, C), jnp.float32)

    def accumulate(total, pair):
        return total + weight_terms(pair[0], pair[1]), None

    grad_two, _ = lax.scan(accumulate, zeros, (padded_hidden, grad_out))
    grad_one, _ = lax.scan(accumulate, zeros, (padded_in, grad_pre))
    return grad_one, grad_two


def reference(features, occupancy, nbr_slots, send_mask, cotangent, weight_one, weight_two):
    zeros = jnp.zeros((C, 27, C), jnp.float32)

    def per_scene(totals, scene):
        first, second = one_scene(scene[0], scene[1], scene[2], scene[3], scene[4], weight_one, weight_two)
        return (totals[0] + first, totals[1] + second), None

    totals, _ = lax.scan(per_scene, (zeros, zeros), (features, occupancy, nbr_slots, send_mask, cotangent))
    return totals[0], totals[1]
```

```python
import jax
import jax.numpy as jnp
import numpy as np
from jax import lax
from jax.experimental import pallas as pl
from jax.experimental.pallas import tpu as pltpu
from jax.sharding import PartitionSpec as P

E = 8
VOX = E**3
C = 256
NX, NY, NZ = 4, 4, 8
BRICKS = NX * NZ
DISTANCES = (-3, -2, -1, 1, 2, 3)
PAY = E * E
OWN = VOX
ROWS = VOX + 6 * PAY
KP = 28
PIECE = KP * 8
SHARE = PIECE // 4
LANES = 128
F32 = jnp.float32
BF16 = jnp.bfloat16
MESH = pl.DeviceIdType.MESH


def offset_index(shift):
    number = (shift[0] + 1) * 9 + (shift[1] + 1) * 3 + (shift[2] + 1)
    return None if number == 13 else (number if number < 13 else number - 1)


def padded_table():
    table = np.zeros((3, 10, 10, 8, 128), np.float32)
    for oc in range(3):
        for a in range(10):
            for b in range(10):
                for c in range(8):
                    at = (a, b, c + oc)
                    shift = [-1 if t == 0 else (1 if t == 9 else 0) for t in at]
                    free = [t - 1 for t, m in zip(at, shift) if m == 0]
                    q = offset_index(shift)
                    line = table[oc, a, b, c]
                    if q is None:
                        line[27] = free[0]
                        line[26] = free[1] * 8 + free[2]
                    else:
                        line[q] = 1
                        row = 0
                        for t in free:
                            row = row * 8 + t
                        line[26] = row
    return table.reshape(3 * 800, 128)


def payload_table():
    hi = np.zeros((PAY, 128), np.float32)
    lo = np.zeros((PAY, 128), np.float32)
    for a in (-1, 0, 1):
        for b in (-1, 0, 1):
            for c in (-1, 0, 1):
                shift = (a, b, c)
                q = offset_index(shift)
                if q is None:
                    continue
                n_free = sum(t == 0 for t in shift)
                for r in range(8**n_free):
                    rest, at = r, [0, 0, 0]
                    for dim in (2, 1, 0):
                        if shift[dim] == 0:
                            at[dim] = rest % 8
                            rest //= 8
                        else:
                            at[dim] = 7 if shift[dim] == 1 else 0
                    hi[r, q] = at[0] + 1
                    lo[r, q] = at[1] * 8 + at[2]
    return np.concatenate([hi, lo], axis=1)


def kernel(
    feat, occ, nbr, send, cot, w1_hbm, w2_hbm, qtab, ptab,
    out,
    w1, w2, nbrv, occb, sel, oh, um, uh, ug, hsend, win_m, win_h, pre, grads,
    psend, precv, asend, arecv, zsend, zrecv, bsend, brecv, gath,
    wsem, hs, hr, ps, pr, as_, ar, zs, zr, bs, br, gs, gr,
):
    d = lax.axis_index("dp")
    s = lax.axis_index("space")
    core = lax.rem(d, 2)
    y = d // 2
    x = lax.rem(s, NX)
    z = s // NX
    not_core = 1 - core
    pa = x * not_core + y * core
    pb = y * not_core + x * core

    def a_dev(j):
        return (d * not_core + (2 * j + core) * core, (z * NX + j) * not_core + s * core)

    def b_dev(j):
        return ((2 * j + core) * not_core + d * core, s * not_core + (z * NX + j) * core)

    def z_dev(j):
        return (d, j * NX + x)

    def group_dev(dy, dc):
        return (lax.rem(y + dy, NY) * 2 + lax.rem(core + dc, 2), s)

    relations = [(dy, dc) for dy in range(NY) for dc in range(2) if dy or dc]

    load1 = pltpu.make_async_copy(w1_hbm, w1, wsem.at[0])
    load1.start()
    load2 = pltpu.make_async_copy(w2_hbm, w2, wsem.at[1])
    load2.start()

    barrier = pltpu.get_barrier_semaphore()
    partners = [group_dev(dy, dc) for dy, dc in relations]
    partners += [(d, z * NX + lax.rem(x + j, NX)) for j in (1, 2, 3)]
    partners += [z_dev(lax.rem(z + 1, NZ)), z_dev(lax.rem(z + NZ - 1, NZ))]
    partners += [(d, lax.rem(s + t + BRICKS, BRICKS)) for t in DISTANCES]
    for partner in partners:
        pl.semaphore_signal(barrier, inc=1, device_id=partner, device_id_type=MESH)

    pending = []

    def push(src, dst, send_sem, recv_sem, dev):
        copy = pltpu.make_async_remote_copy(
            src_ref=src, dst_ref=dst, send_sem=send_sem, recv_sem=recv_sem,
            device_id=dev, device_id_type=MESH,
        )
        copy.start()
        pending.append(copy)
        return copy

    occ_row = jnp.broadcast_to(occ[...].astype(F32), (LANES, VOX))
    for j in range(VOX // LANES):
        occb[pl.ds(j * LANES, LANES), :] = occ_row[:, j * LANES : (j + 1) * LANES].T

    def occupied():
        return jnp.concatenate([occb[...], occb[...]], axis=1)

    um[pl.ds(0, OWN), :] = (feat[...].astype(F32) * occupied()).astype(BF16)

    nbrv[...] = jnp.full((1, 128), -1, jnp.int32)
    nbrv[:, 0:26] = nbr[...]
    slots = nbrv[...]
    scale = jnp.where(lax.broadcasted_iota(jnp.int32, (256, 128), 0) < 128, 64.0, 1.0).astype(BF16)
    lane = lax.broadcasted_iota(jnp.int32, (PAY, 128), 1)
    for t in range(6):
        flag = send[0, t].astype(F32)
        chosen = jnp.where(slots == t, flag, 0.0)
        rows = ptab[...] * jnp.concatenate([chosen, chosen], axis=1)
        voxel = jnp.dot(rows.astype(BF16), scale, preferred_element_type=F32).astype(jnp.int32)
        for j in range(VOX // LANES):
            hit = voxel == lane + (64 + j * LANES)
            sel[pl.ds(t * PAY, PAY), pl.ds(j * LANES, LANES)] = jnp.where(hit, 1.0, 0.0).astype(BF16)

    pl.semaphore_wait(barrier, len(partners))

    def send_halo(which, field):
        packed = jnp.dot(sel[...], field[pl.ds(0, OWN), :], preferred_element_type=F32)
        hsend[which] = packed.astype(BF16)
        return [
            push(
                hsend.at[which, pl.ds(t * PAY, PAY)],
                field.at[pl.ds(OWN + (5 - t) * PAY, PAY)],
                hs.at[which, t],
                hr.at[which, 5 - t],
                (d, lax.rem(s + DISTANCES[t] + BRICKS, BRICKS)),
            )
            for t in range(6)
        ]

    sent = send_halo(0, um)

    distance = jnp.where(slots < 3, slots - 3, slots - 2)
    other = s + distance
    present = (slots >= 0) & (slots < 6) & (other >= 0) & (other < BRICKS)
    base = jnp.where(present, 64 * (8 + slots), 64 * 32).astype(F32)
    lane1 = lax.broadcasted_iota(jnp.int32, (1, 128), 1)
    base = jnp.where(lane1 < 26, base, jnp.where(lane1 == 26, 1.0, jnp.where(lane1 == 27, 64.0, 0.0)))
    ones = jnp.ones((128, 128), BF16)

    def lay(i, carry):
        at = pl.multiple_of(i * 80, 16)
        rows = qtab[pl.ds(at, 80), :].astype(F32) * base
        source = jnp.dot(rows.astype(BF16), ones, preferred_element_type=F32).astype(jnp.int32)
        lanes80 = lax.broadcasted_iota(jnp.int32, (80, 128), 1)
        for j in range(ROWS // LANES):
            hit = source == lanes80 + j * LANES
            oh[pl.ds(at, 80), pl.ds(j * LANES, LANES)] = jnp.where(hit, 1.0, 0.0).astype(BF16)
        return carry

    lax.fori_loop(0, 30, lay, 0)

    def build_windows(field, win):
        def one(oc, carry):
            for half in range(2):
                rows = oh[pl.ds(pl.multiple_of(oc * 800 + half * 400, 16), 400), :]
                padded = jnp.dot(rows, field[...], preferred_element_type=F32).reshape(5, 80, C)
                for ob in range(3):
                    part = padded[:, ob * 8 : ob * 8 + 64].reshape(320, C).astype(BF16)
                    lanes = pl.ds(pl.multiple_of((ob * 3 + oc) * C, C), C)
                    win[pl.ds(half * 320, 320), lanes] = part
            return carry

        lax.fori_loop(0, 3, one, 0)

    def conv(win, weight):
        for m in range(2):
            acc = jnp.zeros((256, C), F32)
            for oa in range(3):
                acc = acc + jnp.dot(
                    win[pl.ds(oa * 64 + m * 256, 256), :],
                    weight[pl.ds(oa * 9 * C, 9 * C), :],
                    preferred_element_type=F32,
                )
            yield m, acc

    def slope(value):
        sig = jax.nn.sigmoid(value)
        return sig * (1.0 + value * (1.0 - sig))

    def half_occ(m):
        part = occb[pl.ds(m * 256, 256), :]
        return jnp.concatenate([part, part], axis=1)

    for copy in sent:
        copy.wait_recv()
    build_windows(um, win_m)
    load1.wait()
    for m, acc in conv(win_m, w1):
        value = acc * half_occ(m)
        pre[pl.ds(m * 256, 256), :] = value
        uh[pl.ds(m * 256, 256), :] = (value * jax.nn.sigmoid(value)).astype(BF16)
    sent = send_halo(1, uh)
    for copy in sent:
        copy.wait_recv()
    build_windows(uh, win_h)
    load2.wait()
    for m, acc in conv(win_h, w2):
        rows = pl.ds(m * 256, 256)
        value = acc * half_occ(m) + um[rows, :].astype(F32)
        ug[rows, :] = (cot[rows, :].astype(F32) * slope(value) * half_occ(m)).astype(BF16)
    sent = send_halo(2, ug)

    def weight_grad(g, win, grad):
        def one(k, carry):
            view = win[
                pl.ds(pl.multiple_of((k // 9) * 64, 64), VOX),
                pl.ds(pl.multiple_of(lax.rem(k, 9) * C, C), C),
            ]
            res = lax.dot_general(view, grad[pl.ds(0, OWN), :], (((0,), (0,)), ((), ())), preferred_element_type=F32)
            res = res.reshape(NZ, NX, 8, C)
            ky = k // 7
            for xx in range(NX):
                grads[g, 0, xx, :, pl.ds(pl.multiple_of(k * 8, 8), 8), :] = res[:, xx, :, :LANES]
                at = pl.multiple_of(xx * SHARE + lax.rem(k, 7) * 8, 8)
                grads[g, 1, ky, :, pl.ds(at, 8), :] = res[:, xx, :, LANES:]
            return carry

        lax.fori_loop(0, 27, one, 0)
        blank = jnp.zeros((NZ, 8, LANES), F32)
        for xx in range(NX):
            grads[g, 0, xx, :, pl.ds(27 * 8, 8), :] = blank
            grads[g, 1, 3, :, pl.ds(xx * SHARE + 48, 8), :] = blank

    def pair_start(g):
        copies = []
        for j, step in enumerate((2, 1, 3, 0)):
            block = lax.rem(pb + step, 4)

            def cast(i, carry):
                psend[g, block, i] = grads[g, not_core, block, i].astype(BF16)
                return carry

            lax.fori_loop(0, NZ, cast, 0)
            copies.append(
                push(psend.at[g, block], precv.at[g, block], ps.at[g, j], pr.at[g, j], (d + not_core - core, s))
            )
        return copies

    right_a, left_a = a_dev(lax.rem(pa + 1, 4)), a_dev(lax.rem(pa + 3, 4))

    def a_push(g, slot, dev):
        return push(asend.at[g, slot], arecv.at[g, slot], as_.at[g, slot], ar.at[g, slot], dev)

    def ring_a_first(g, pairs):
        opposite, right, left = lax.rem(pa + 2, 4), lax.rem(pa + 1, 4), lax.rem(pa + 3, 4)
        copies = [None] * 6

        def fold(block):
            def add(i, carry):
                grads[g, core, block, i] = grads[g, core, block, i] + precv[g, block, i].astype(F32)
                return carry

            lax.fori_loop(0, NZ, add, 0)

        def stage(slot, block, lo):
            def cast(i, carry):
                asend[g, slot, i] = grads[g, core, block, lo + i].astype(BF16)
                return carry

            lax.fori_loop(0, 4, cast, 0)

        pairs[0].wait_recv()
        fold(opposite)
        stage(0, opposite, 0)
        copies[0] = a_push(g, 0, right_a)
        stage(1, opposite, 4)
        copies[1] = a_push(g, 1, left_a)
        pairs[1].wait_recv()
        fold(right)
        stage(2, right, 4)
        copies[2] = a_push(g, 2, right_a)
        pairs[2].wait_recv()
        fold(left)
        stage(3, left, 0)
        copies[3] = a_push(g, 3, left_a)
        pairs[3].wait_recv()
        fold(pa)
        return copies

    def ring_a_second(g, copies):
        right, left = lax.rem(pa + 1, 4), lax.rem(pa + 3, 4)
        for slot, block, lo, dev in ((4, right, 0, right_a), (5, left, 4, left_a)):
            copies[slot - 4].wait_recv()

            def add(i, carry):
                total = grads[g, core, block, lo + i] + arecv[g, slot - 4, i].astype(F32)
                asend[g, slot, i] = total.astype(BF16)
                return carry

            lax.fori_loop(0, 4, add, 0)
            copies[slot] = a_push(g, slot, dev)

    def ring_a_last(g, copies):
        for slot in (2, 3, 4, 5):
            copies[slot].wait_recv()

        def add(i, carry):
            low = arecv[g, 4, i].astype(F32) + arecv[g, 3, i].astype(F32)
            grads[g, core, pa, i] = grads[g, core, pa, i] + low
            high = arecv[g, 2, i].astype(F32) + arecv[g, 5, i].astype(F32)
            grads[g, core, pa, i + 4] = grads[g, core, pa, i + 4] + high
            return carry

        lax.fori_loop(0, 4, add, 0)

    sides = (z_dev(lax.rem(z + 1, NZ)), z_dev(lax.rem(z + NZ - 1, NZ)))
    HALF = PIECE // 2

    def ring_z_step(g, step, before):
        copies = []
        for way in range(2):
            hop = 4 - step
            block = lax.rem(z + (hop if way == 0 else NZ - hop), NZ)
            mine = pl.ds(way * HALF, HALF)
            if step == 0:
                zsend[g, way, 0, mine, :] = grads[g, core, pa, block, mine, :].astype(BF16)
                part = mine
            else:
                before[way].wait_recv()
                if step == 1:
                    rest = pl.ds((1 - way) * HALF, HALF)
                    zsend[g, way, 1, rest, :] = grads[g, core, pa, block, rest, :].astype(BF16)
                    total = grads[g, core, pa, block, mine, :] + zrecv[g, way, 0, mine, :].astype(F32)
                    zsend[g, way, 1, mine, :] = total.astype(BF16)
                else:
                    total = grads[g, core, pa, block] + zrecv[g, way, step - 1].astype(F32)
                    zsend[g, way, step] = total.astype(BF16)
                part = pl.ds(0, PIECE)
            copies.append(
                push(
                    zsend.at[g, way, step, part],
                    zrecv.at[g, way, step, part],
                    zs.at[g, way, step],
                    zr.at[g, way, step],
                    sides[way],
                )
            )
        return copies

    def ring_b_start(g, before):
        for copy in before:
            copy.wait_recv()
        total = grads[g, core, pa, z] + (zrecv[g, 0, 3].astype(F32) + zrecv[g, 1, 3].astype(F32))
        bsend[g] = total
        copies = []
        for j in (1, 2, 3):
            to = lax.rem(pb + j, 4)
            copies.append(
                push(
                    bsend.at[g, pl.ds(pl.multiple_of(to * SHARE, 8), SHARE)],
                    brecv.at[g, j - 1],
                    bs.at[g, j - 1],
                    br.at[g, j - 1],
                    b_dev(to),
                )
            )
        return copies

    def gather_start(g, before):
        for copy in before:
            copy.wait_recv()
        total = bsend[g, pl.ds(pl.multiple_of(pb * SHARE, 8), SHARE), :]
        for j in range(3):
            total = total + brecv[g, j]
        gath[g, y, core] = total
        return [
            push(gath.at[g, y, core], gath.at[g, y, core], gs.at[g, n], gr.at[g, n], group_dev(dy, dc))
            for n, (dy, dc) in enumerate(relations)
        ]

    weight_grad(0, win_h, ug)
    pairs_two = pair_start(0)

    for copy in sent:
        copy.wait_recv()
    build_windows(ug, win_h)
    ring_two = ring_a_first(0, pairs_two)
    for m in range(2):
        acc = jnp.zeros((256, C), F32)
        for oa in range(3):
            weights = jnp.concatenate([w2[pl.ds((26 - oa * 9 - j) * C, C), :] for j in range(9)], axis=1)
            acc = acc + lax.dot_general(
                win_h[pl.ds(oa * 64 + m * 256, 256), :],
                weights,
                (((1,), (1,)), ((), ())),
                preferred_element_type=F32,
            )
        rows = pl.ds(m * 256, 256)
        uh[rows, :] = (acc * slope(pre[rows, :]) * half_occ(m)).astype(BF16)
    ring_a_second(0, ring_two)

    weight_grad(1, win_m, uh)
    pairs_one = pair_start(1)
    ring_a_last(0, ring_two)
    steps = ring_z_step(0, 0, None)
    ring_one = ring_a_first(1, pairs_one)
    steps = ring_z_step(0, 1, steps)
    ring_a_second(1, ring_one)
    steps = ring_z_step(0, 2, steps)
    steps = ring_z_step(0, 3, steps)
    steps = ring_b_start(0, steps)
    done_two = gather_start(0, steps)
    ring_a_last(1, ring_one)
    steps = None
    for step in range(4):
        steps = ring_z_step(1, step, steps)
    steps = ring_b_start(1, steps)
    done_one = gather_start(1, steps)
    for copy in done_two + done_one:
        copy.wait_recv()
    out[...] = gath[...]
    for copy in pending:
        copy.wait_send()


def local(features, occupancy, nbr_slots, send_mask, cotangent, weight_one, weight_two):
    vmem = pl.BlockSpec(memory_space=pltpu.VMEM)
    smem = pl.BlockSpec(memory_space=pltpu.SMEM)
    hbm = pl.BlockSpec(memory_space=pl.ANY)
    dma = pltpu.SemaphoreType.DMA
    res = pl.pallas_call(
        kernel,
        out_shape=jax.ShapeDtypeStruct((2, NY, 2, SHARE, LANES), F32),
        in_specs=[vmem, vmem, vmem, smem, vmem, hbm, hbm, vmem, vmem],
        out_specs=vmem,
        scratch_shapes=[
            pltpu.VMEM((27 * C, C), BF16),
            pltpu.VMEM((27 * C, C), BF16),
            pltpu.VMEM((1, 128), jnp.int32),
            pltpu.VMEM((VOX, LANES), F32),
            pltpu.VMEM((6 * PAY, VOX), BF16),
            pltpu.VMEM((2400, ROWS), BF16),
            pltpu.VMEM((ROWS, C), BF16),
            pltpu.VMEM((ROWS, C), BF16),
            pltpu.VMEM((ROWS, C), BF16),
            pltpu.VMEM((3, 6 * PAY, C), BF16),
            pltpu.VMEM((640, 9 * C), BF16),
            pltpu.VMEM((640, 9 * C), BF16),
            pltpu.VMEM((VOX, C), F32),
            pltpu.VMEM((2, 2, 4, NZ, PIECE, LANES), F32),
            pltpu.VMEM((2, 4, NZ, PIECE, LANES), BF16),
            pltpu.VMEM((2, 4, NZ, PIECE, LANES), BF16),
            pltpu.VMEM((2, 6, 4, PIECE, LANES), BF16),
            pltpu.VMEM((2, 6, 4, PIECE, LANES), BF16),
            pltpu.VMEM((2, 2, 4, PIECE, LANES), BF16),
            pltpu.VMEM((2, 2, 4, PIECE, LANES), BF16),
            pltpu.VMEM((2, PIECE, LANES), F32),
            pltpu.VMEM((2, 3, SHARE, LANES), F32),
            pltpu.VMEM((2, NY, 2, SHARE, LANES), F32),
            dma((2,)),
            dma((3, 6)),
            dma((3, 6)),
            dma((2, 4)),
            dma((2, 4)),
            dma((2, 6)),
            dma((2, 6)),
            dma((2, 2, 4)),
            dma((2, 2, 4)),
            dma((2, 3)),
            dma((2, 3)),
            dma((2, 7)),
            dma((2, 7)),
        ],
        compiler_params=pltpu.CompilerParams(
            collective_id=0, has_side_effects=True, vmem_limit_bytes=60 * 1024 * 1024
        ),
    )(
        features.reshape(VOX, C),
        occupancy.reshape(1, VOX),
        nbr_slots.reshape(1, 26),
        send_mask.reshape(1, 6),
        cotangent.reshape(VOX, C),
        weight_one.reshape(27 * C, C),
        weight_two.reshape(27 * C, C),
        jnp.asarray(padded_table(), BF16),
        jnp.asarray(payload_table(), F32),
    )
    res = res.reshape(2, NY, 2, 7, 8, LANES).transpose(0, 4, 1, 3, 2, 5).reshape(2, 8, KP, C)[:, :, :27]
    return res[1], res[0]


def solution(mesh):
    in_specs = (
        P("dp", "space", None, None),
        P("dp", "space", None),
        P("dp", "space", None),
        P("dp", "space", None),
        P("dp", "space", None, None),
        P(),
        P(),
    )
    out_specs = (P("space", None, None), P("space", None, None))
    return jax.shard_map(local, mesh=mesh, in_specs=in_specs, out_specs=out_specs, check_vma=False)
```

```python
import jax
import jax.numpy as jnp
import numpy as np
from jax import lax
from jax.experimental import pallas as pl
from jax.experimental.pallas import tpu as pltpu
from jax.sharding import PartitionSpec as P

E = 8
VOX = E**3
C = 256
NX, NY, NZ = 4, 4, 8
BRICKS = NX * NZ
DISTANCES = (-3, -2, -1, 1, 2, 3)
PAY = E * E
OWN = VOX
ROWS = VOX + 6 * PAY
KP = 28
UNITS = 14
UNROLL = 4
FLOWS = ((0, 6), (6, 4), (10, 2), (12, 2))
ROWS_ALL = UNITS * 4 * 8
LANES = 128
F32 = jnp.float32
BF16 = jnp.bfloat16
MESH = pl.DeviceIdType.MESH


def offset_index(shift):
    number = (shift[0] + 1) * 9 + (shift[1] + 1) * 3 + (shift[2] + 1)
    return None if number == 13 else (number if number < 13 else number - 1)


def padded_table():
    table = np.zeros((3, 10, 10, 8, 128), np.float32)
    for oc in range(3):
        for a in range(10):
            for b in range(10):
                for c in range(8):
                    at = (a, b, c + oc)
                    shift = [-1 if t == 0 else (1 if t == 9 else 0) for t in at]
                    free = [t - 1 for t, m in zip(at, shift) if m == 0]
                    q = offset_index(shift)
                    line = table[oc, a, b, c]
                    if q is None:
                        line[27] = free[0]
                        line[26] = free[1] * 8 + free[2]
                    else:
                        line[q] = 1
                        row = 0
                        for t in free:
                            row = row * 8 + t
                        line[26] = row
    return table.reshape(3 * 800, 128)


def payload_table():
    hi = np.zeros((PAY, 128), np.float32)
    lo = np.zeros((PAY, 128), np.float32)
    for a in (-1, 0, 1):
        for b in (-1, 0, 1):
            for c in (-1, 0, 1):
                shift = (a, b, c)
                q = offset_index(shift)
                if q is None:
                    continue
                n_free = sum(t == 0 for t in shift)
                for r in range(8**n_free):
                    rest, at = r, [0, 0, 0]
                    for dim in (2, 1, 0):
                        if shift[dim] == 0:
                            at[dim] = rest % 8
                            rest //= 8
                        else:
                            at[dim] = 7 if shift[dim] == 1 else 0
                    hi[r, q] = at[0] + 1
                    lo[r, q] = at[1] * 8 + at[2]
    return np.concatenate([hi, lo], axis=1)


def kernel(
    feat_hbm, occ, nbr, send, cot_hbm, w1_hbm, w2_hbm, qtab_hbm, ptab_hbm,
    out,
    feat, cot, qtab, ptab, w1, w2, nbrv, occb, sel, oh, um, uh, ug, hsend, win_m, win_h, tm, th, gpad, pre, grads,
    psend, precv, asend, arecv, zsend, zrecv, gath,
    wsem, hs, hr, ps, pr, as_, ar, zs, zr, gs, gr,
):
    d = lax.axis_index("dp")
    s = lax.axis_index("space")
    core = lax.rem(d, 2)
    y = d // 2
    x = lax.rem(s, NX)
    z = s // NX
    not_core = 1 - core
    pa = x * not_core + y * core
    pb = y * not_core + x * core

    near_x = [x] + [lax.rem(x + j, NX) for j in range(1, NX)]
    near_y = [y] + [lax.rem(y + j, NY) for j in range(1, NY)]
    near_z = [z] + [lax.rem(z + j, NZ) for j in range(1, NZ)]
    near_a = [i * not_core + j * core for i, j in zip(near_x, near_y)]
    near_b = [j * not_core + i * core for i, j in zip(near_x, near_y)]
    row_y = [2 * j + core for j in near_y]
    ring_dev = [(d * not_core + row_y[j] * core, z * NX + (near_x[j] * not_core + x * core)) for j in range(4)]
    b_dp = [row_y[j] * not_core + d * core for j in range(4)]
    b_sp = [x * not_core + near_x[j] * core for j in range(4)]
    row_z = [j * NX for j in near_z]

    def plane_dev(j):
        return (b_dp[j % 4], row_z[j // 4] + b_sp[j % 4])

    def group_dev(dy, dc):
        return (2 * near_y[dy] + (not_core if dc else core), s)

    relations = [(dy, dc) for dy in range(NY) for dc in range(2) if dy or dc]

    loads = []
    for n, (src, dst) in enumerate(
        ((ptab_hbm, ptab), (feat_hbm, feat), (qtab_hbm, qtab), (w1_hbm, w1), (cot_hbm, cot), (w2_hbm, w2))
    ):
        loads.append(pltpu.make_async_copy(src, dst, wsem.at[n]))
        loads[-1].start()

    barrier = pltpu.get_barrier_semaphore()
    partners = [group_dev(dy, dc) for dy, dc in relations]
    partners += [ring_dev[j] for j in (1, 2, 3)]
    partners += [plane_dev(j) for j in range(1, 32)]
    partners += [(d, lax.rem(s + t + BRICKS, BRICKS)) for t in DISTANCES]
    for partner in partners:
        pl.semaphore_signal(barrier, inc=1, device_id=partner, device_id_type=MESH)

    pending = []

    def push(src, dst, send_sem, recv_sem, dev):
        copy = pltpu.make_async_remote_copy(
            src_ref=src, dst_ref=dst, send_sem=send_sem, recv_sem=recv_sem,
            device_id=dev, device_id_type=MESH,
        )
        copy.start()
        pending.append(copy)
        return copy

    occ_row = jnp.broadcast_to(occ[...].astype(F32), (LANES, VOX))
    for j in range(VOX // LANES):
        occb[pl.ds(j * LANES, LANES), :] = occ_row[:, j * LANES : (j + 1) * LANES].T

    def occupied():
        return jnp.concatenate([occb[...], occb[...]], axis=1)

    loads[1].wait()
    um[pl.ds(0, OWN), :] = (feat[...].astype(F32) * occupied()).astype(BF16)

    nbrv[...] = jnp.full((1, 128), -1, jnp.int32)
    nbrv[:, 0:26] = nbr[...]
    slots = nbrv[...]
    scale = jnp.where(lax.broadcasted_iota(jnp.int32, (256, 128), 0) < 128, 64.0, 1.0).astype(BF16)
    lane = lax.broadcasted_iota(jnp.int32, (PAY, 128), 1)
    loads[0].wait()
    for t in range(6):
        flag = send[0, t].astype(F32)
        chosen = jnp.where(slots == t, flag, 0.0)
        rows = ptab[...] * jnp.concatenate([chosen, chosen], axis=1)
        voxel = jnp.dot(rows.astype(BF16), scale, preferred_element_type=F32).astype(jnp.int32)
        for j in range(VOX // LANES):
            hit = voxel == lane + (64 + j * LANES)
            sel[pl.ds(t * PAY, PAY), pl.ds(j * LANES, LANES)] = jnp.where(hit, 1.0, 0.0).astype(BF16)

    pl.semaphore_wait(barrier, len(partners))

    def send_halo(which, field):
        packed = jnp.dot(sel[...], field[pl.ds(0, OWN), :], preferred_element_type=F32)
        hsend[which] = packed.astype(BF16)
        return [
            push(
                hsend.at[which, pl.ds(t * PAY, PAY)],
                field.at[pl.ds(OWN + (5 - t) * PAY, PAY)],
                hs.at[which, t],
                hr.at[which, 5 - t],
                (d, lax.rem(s + DISTANCES[t] + BRICKS, BRICKS)),
            )
            for t in range(6)
        ]

    sent = send_halo(0, um)

    distance = jnp.where(slots < 3, slots - 3, slots - 2)
    other = s + distance
    present = (slots >= 0) & (slots < 6) & (other >= 0) & (other < BRICKS)
    base = jnp.where(present, 64 * (8 + slots), 64 * 32).astype(F32)
    lane1 = lax.broadcasted_iota(jnp.int32, (1, 128), 1)
    base = jnp.where(lane1 < 26, base, jnp.where(lane1 == 26, 1.0, jnp.where(lane1 == 27, 64.0, 0.0)))
    ones = jnp.ones((128, 128), BF16)

    def lay(i, carry):
        at = pl.multiple_of(i * 80, 16)
        rows = qtab[pl.ds(at, 80), :].astype(F32) * base
        source = jnp.dot(rows.astype(BF16), ones, preferred_element_type=F32).astype(jnp.int32)
        lanes80 = lax.broadcasted_iota(jnp.int32, (80, 128), 1)
        for j in range(ROWS // LANES):
            hit = source == lanes80 + j * LANES
            oh[pl.ds(at, 80), pl.ds(j * LANES, LANES)] = jnp.where(hit, 1.0, 0.0).astype(BF16)
        return carry

    loads[2].wait()
    lax.fori_loop(0, 30, lay, 0)

    def build_windows(field, win):
        def one(oc, carry):
            for half in range(2):
                rows = oh[pl.ds(pl.multiple_of(oc * 800 + half * 400, 16), 400), :]
                padded = jnp.dot(rows, field[...], preferred_element_type=F32).reshape(5, 80, C)
                for ob in range(3):
                    part = padded[:, ob * 8 : ob * 8 + 64].reshape(320, C).astype(BF16)
                    lanes = pl.ds(pl.multiple_of((ob * 3 + oc) * C, C), C)
                    win[pl.ds(half * 320, 320), lanes] = part
            return carry

        lax.fori_loop(0, 3, one, 0)

    def conv(win, weight):
        for m in range(2):
            acc = jnp.zeros((256, C), F32)
            for oa in range(3):
                acc = acc + jnp.dot(
                    win[pl.ds(oa * 64 + m * 256, 256), :],
                    weight[pl.ds(oa * 9 * C, 9 * C), :],
                    preferred_element_type=F32,
                )
            yield m, acc

    def slope(value):
        sig = jax.nn.sigmoid(value)
        return sig * (1.0 + value * (1.0 - sig))

    def half_occ(m):
        part = occb[pl.ds(m * 256, 256), :]
        return jnp.concatenate([part, part], axis=1)

    def transpose_windows(win, turned):
        def one(j, carry):
            at = pl.ds(pl.multiple_of(j * C, C), C)
            turned[at, :] = win[:, at].T
            return carry

        lax.fori_loop(0, 9, one, 0)

    gpad[pl.ds(0, 64), :] = jnp.zeros((64, C), BF16)
    gpad[pl.ds(576, 64), :] = jnp.zeros((64, C), BF16)

    for copy in sent:
        copy.wait_recv()
    build_windows(um, win_m)
    loads[3].wait()
    for m, acc in conv(win_m, w1):
        value = acc * half_occ(m)
        pre[pl.ds(m * 256, 256), :] = value
        uh[pl.ds(m * 256, 256), :] = (value * jax.nn.sigmoid(value)).astype(BF16)
    sent = send_halo(1, uh)
    transpose_windows(win_m, tm)
    for copy in sent:
        copy.wait_recv()
    build_windows(uh, win_h)
    loads[4].wait()
    loads[5].wait()
    for m, acc in conv(win_h, w2):
        rows = pl.ds(m * 256, 256)
        value = acc * half_occ(m) + um[rows, :].astype(F32)
        grad = (cot[rows, :].astype(F32) * slope(value) * half_occ(m)).astype(BF16)
        ug[rows, :] = grad
        gpad[pl.ds(64 + m * 256, 256), :] = grad
    sent = send_halo(2, ug)
    transpose_windows(win_h, th)

    def weight_grad(unit, turned):
        k7 = unit % 7
        for ky in range(4):
            k = ky * 7 + k7
            if k < 27:
                rows = pl.ds((k % 9) * C, C)
                if k // 9 == 1:
                    left, right = turned[rows, :], gpad[...]
                else:
                    left, right = turned[rows, pl.ds((k // 9) * 64, VOX)], gpad[pl.ds(64, VOX), :]
                res = jnp.dot(left, right, preferred_element_type=F32).reshape(NZ, NX, 8, C)
            else:
                res = jnp.zeros((NZ, NX, 8, C), F32)
            for xx in range(NX):
                grads[0, xx, :, pl.ds(unit_row(unit, ky), 8), :] = res[:, xx, :, :LANES]
                grads[1, ky, :, pl.ds(unit_row(unit, xx), 8), :] = res[:, xx, :, LANES:]

    def unit_row(unit, b):
        lo, n = next(f for f in FLOWS if f[0] <= unit < f[0] + f[1])
        return lo * 32 + b * n * 8 + (unit - lo) * 8

    def pair_start(f):
        lo, n = FLOWS[f]
        part = pl.ds(lo * 32, n * 32)
        copies = []
        for j in range(4):
            block = near_b[(j + 1) % 4]

            def cast(i, carry):
                psend[block, i, part, :] = grads[not_core, block, i, part, :].astype(BF16)
                return carry

            lax.fori_loop(0, NZ, cast, 0, unroll=UNROLL)
            copies.append(
                push(
                    psend.at[block, :, part],
                    precv.at[block, :, part],
                    ps.at[f, j],
                    pr.at[f, j],
                    (d + not_core - core, s),
                )
            )
        return copies

    def ring_start(f, pairs):
        lo, n = FLOWS[f]
        part = pl.ds(lo * 32, n * 32)
        copies = []
        for j in range(4):
            block = near_a[(j + 1) % 4]
            pairs[j].wait_recv()

            def add(i, carry):
                total = grads[core, block, i, part, :] + precv[block, i, part, :].astype(F32)
                if j < 3:
                    asend[j, i, part, :] = total.astype(BF16)
                else:
                    grads[core, pa, i, part, :] = total
                return carry

            lax.fori_loop(0, NZ, add, 0, unroll=UNROLL)
            if j < 3:
                copies.append(
                    push(asend.at[j, :, part], arecv.at[j, :, part], as_.at[f, j], ar.at[f, j], ring_dev[j + 1])
                )
        return copies

    def plane_copy(f, j):
        lo, n = FLOWS[f]
        rows = pl.ds(pl.multiple_of(lo * 32 + near_b[j % 4] * (n * 8), 16), n * 8)
        return pltpu.make_async_remote_copy(
            src_ref=zsend.at[near_z[j // 4], rows],
            dst_ref=zrecv.at[j, pl.ds(lo * 8, n * 8)],
            send_sem=zs.at[f],
            recv_sem=zr.at[f],
            device_id=plane_dev(j),
            device_id_type=MESH,
        )

    def plane_all(f, sem):
        lo, n = FLOWS[f]
        here = zrecv.at[pl.ds(1, 31), pl.ds(lo * 8, n * 8)]
        return pltpu.make_async_copy(here, here, sem.at[f])

    def plane_start(f, before):
        lo, n = FLOWS[f]
        part = pl.ds(lo * 32, n * 32)
        for copy in before:
            copy.wait_recv()

        def add(i, carry):
            far = arecv[0, i, part, :].astype(F32) + arecv[1, i, part, :].astype(F32)
            total = grads[core, pa, i, part, :] + (far + arecv[2, i, part, :].astype(F32))
            grads[core, pa, i, part, :] = total
            zsend[i, part, :] = total.astype(BF16)
            return carry

        lax.fori_loop(0, NZ, add, 0, unroll=UNROLL)

        for j in range(1, 32):
            plane_copy(f, j).start()

    def gather_start(f):
        lo, n = FLOWS[f]
        part = pl.ds(lo * 8, n * 8)
        mine = pl.ds(pl.multiple_of(lo * 32 + pb * (n * 8), 8), n * 8)

        plane_all(f, zr).wait()
        total = grads[core, pa, z, mine, :]
        for j in range(1, 32):
            total = total + zrecv[j, part, :].astype(F32)
        gath[y, core, part, :] = total
        here = gath.at[y, core, part]
        return [
            push(here, here, gs.at[f, n_], gr.at[f, n_], group_dev(dy, dc))
            for n_, (dy, dc) in enumerate(relations)
        ]

    flow = [None] * len(FLOWS)

    def pair(f):
        flow[f] = pair_start(f)

    def ring(f):
        flow[f] = ring_start(f, flow[f])

    def plane(f):
        plane_start(f, flow[f])
        flow[f] = []

    def gather(f):
        flow[f] = gather_start(f)

    def units(f, which):
        lo, n = FLOWS[f]
        for unit in range(lo, lo + n):
            if unit // 7 == which:
                weight_grad(unit, (th, tm)[which])

    units(0, 0)
    pair(0)
    units(1, 0)
    ring(0)

    for copy in sent:
        copy.wait_recv()
    build_windows(ug, win_h)

    for m in range(2):
        acc = jnp.zeros((256, C), F32)
        for oa in range(3):
            weights = jnp.concatenate([w2[pl.ds((26 - oa * 9 - j) * C, C), :] for j in range(9)], axis=1)
            acc = acc + lax.dot_general(
                win_h[pl.ds(oa * 64 + m * 256, 256), :],
                weights,
                (((1,), (1,)), ((), ())),
                preferred_element_type=F32,
            )
        rows = pl.ds(m * 256, 256)
        gpad[pl.ds(64 + m * 256, 256), :] = (acc * slope(pre[rows, :]) * half_occ(m)).astype(BF16)
    units(1, 1)
    pair(1)
    units(2, 1)
    pair(2)
    ring(1)
    plane(0)
    units(3, 1)
    pair(3)
    ring(2)
    plane(1)
    ring(3)
    gather(0)
    plane(2)
    plane(3)
    gather(1)
    gather(2)
    gather(3)
    for copies in flow:
        for copy in copies:
            copy.wait_recv()
    out[...] = gath[...]
    for copy in pending:
        copy.wait_send()
    for f in range(len(FLOWS)):
        plane_all(f, zs).wait()


def local(features, occupancy, nbr_slots, send_mask, cotangent, weight_one, weight_two):
    vmem = pl.BlockSpec(memory_space=pltpu.VMEM)
    smem = pl.BlockSpec(memory_space=pltpu.SMEM)
    hbm = pl.BlockSpec(memory_space=pl.ANY)
    dma = pltpu.SemaphoreType.DMA
    res = pl.pallas_call(
        kernel,
        out_shape=jax.ShapeDtypeStruct((NY, 2, UNITS * 8, LANES), F32),
        in_specs=[hbm, vmem, vmem, smem, hbm, hbm, hbm, hbm, hbm],
        out_specs=vmem,
        scratch_shapes=[
            pltpu.VMEM((VOX, C), BF16),
            pltpu.VMEM((VOX, C), BF16),
            pltpu.VMEM((2400, 128), BF16),
            pltpu.VMEM((PAY, 256), F32),
            pltpu.VMEM((27 * C, C), BF16),
            pltpu.VMEM((27 * C, C), BF16),
            pltpu.VMEM((1, 128), jnp.int32),
            pltpu.VMEM((VOX, LANES), F32),
            pltpu.VMEM((6 * PAY, VOX), BF16),
            pltpu.VMEM((2400, ROWS), BF16),
            pltpu.VMEM((ROWS, C), BF16),
            pltpu.VMEM((ROWS, C), BF16),
            pltpu.VMEM((ROWS, C), BF16),
            pltpu.VMEM((3, 6 * PAY, C), BF16),
            pltpu.VMEM((640, 9 * C), BF16),
            pltpu.VMEM((640, 9 * C), BF16),
            pltpu.VMEM((9 * C, 640), BF16),
            pltpu.VMEM((9 * C, 640), BF16),
            pltpu.VMEM((640, C), BF16),
            pltpu.VMEM((VOX, C), F32),
            pltpu.VMEM((2, 4, NZ, ROWS_ALL, LANES), F32),
            pltpu.VMEM((4, NZ, ROWS_ALL, LANES), BF16),
            pltpu.VMEM((4, NZ, ROWS_ALL, LANES), BF16),
            pltpu.VMEM((3, NZ, ROWS_ALL, LANES), BF16),
            pltpu.VMEM((3, NZ, ROWS_ALL, LANES), BF16),
            pltpu.VMEM((NZ, ROWS_ALL, LANES), BF16),
            pltpu.VMEM((32, UNITS * 8, LANES), BF16),
            pltpu.VMEM((NY, 2, UNITS * 8, LANES), F32),
            dma((6,)),
            dma((3, 6)),
            dma((3, 6)),
            dma((len(FLOWS), 4)),
            dma((len(FLOWS), 4)),
            dma((len(FLOWS), 3)),
            dma((len(FLOWS), 3)),
            dma((len(FLOWS),)),
            dma((len(FLOWS),)),
            dma((len(FLOWS), 7)),
            dma((len(FLOWS), 7)),
        ],
        compiler_params=pltpu.CompilerParams(
            collective_id=0, has_side_effects=True, vmem_limit_bytes=60 * 1024 * 1024
        ),
    )(
        features.reshape(VOX, C),
        occupancy.reshape(1, VOX),
        nbr_slots.reshape(1, 26),
        send_mask.reshape(1, 6),
        cotangent.reshape(VOX, C),
        weight_one.reshape(27 * C, C),
        weight_two.reshape(27 * C, C),
        jnp.asarray(padded_table(), BF16),
        jnp.asarray(payload_table(), F32),
    )
    res = res.reshape(NY, 2, 2, 7, 8, LANES).transpose(2, 4, 0, 3, 1, 5).reshape(2, 8, KP, C)[:, :, :27]
    return res[1], res[0]


def solution(mesh):
    in_specs = (
        P("dp", "space", None, None),
        P("dp", "space", None),
        P("dp", "space", None),
        P("dp", "space", None),
        P("dp", "space", None, None),
        P(),
        P(),
    )
    out_specs = (P("space", None, None), P("space", None, None))
    return jax.shard_map(local, mesh=mesh, in_specs=in_specs, out_specs=out_specs, check_vma=False)
```

```python
import jax
import jax.numpy as jnp
import numpy as np
from jax import lax
from jax.experimental import pallas as pl
from jax.experimental.pallas import tpu as pltpu
from jax.sharding import PartitionSpec as P

E = 8
VOX = E**3
C = 256
NX, NY, NZ = 4, 4, 8
BRICKS = NX * NZ
DISTANCES = (-3, -2, -1, 1, 2, 3)
PAY = E * E
OWN = VOX
ROWS = VOX + 6 * PAY
KP = 28
SPLIT = 2
UNITS = 14
UNROLL = 4
FLOWS = ((0, 2), (2, 4), (6, 4), (10, 2), (12, 2))
ROWS_ALL = UNITS * 4 * 8
LANES = 128
F32 = jnp.float32
BF16 = jnp.bfloat16
MESH = pl.DeviceIdType.MESH


def offset_index(shift):
    number = (shift[0] + 1) * 9 + (shift[1] + 1) * 3 + (shift[2] + 1)
    return None if number == 13 else (number if number < 13 else number - 1)


def padded_table():
    table = np.zeros((3, 10, 10, 8, 128), np.float32)
    for oc in range(3):
        for a in range(10):
            for b in range(10):
                for c in range(8):
                    at = (a, b, c + oc)
                    shift = [-1 if t == 0 else (1 if t == 9 else 0) for t in at]
                    free = [t - 1 for t, m in zip(at, shift) if m == 0]
                    q = offset_index(shift)
                    line = table[oc, a, b, c]
                    if q is None:
                        line[27] = free[0]
                        line[26] = free[1] * 8 + free[2]
                    else:
                        line[q] = 1
                        row = 0
                        for t in free:
                            row = row * 8 + t
                        line[26] = row
    return table.reshape(3 * 800, 128)


def own_table():
    table = padded_table()
    own = ~(table[:, :26] != 0).any(axis=1)
    source = np.where(own, 64 * table[:, 27] + table[:, 26], -1)
    return (source[:, None] == np.arange(OWN)[None, :]).astype(np.float32)


def payload_table():
    hi = np.zeros((PAY, 128), np.float32)
    lo = np.zeros((PAY, 128), np.float32)
    for a in (-1, 0, 1):
        for b in (-1, 0, 1):
            for c in (-1, 0, 1):
                shift = (a, b, c)
                q = offset_index(shift)
                if q is None:
                    continue
                n_free = sum(t == 0 for t in shift)
                for r in range(8**n_free):
                    rest, at = r, [0, 0, 0]
                    for dim in (2, 1, 0):
                        if shift[dim] == 0:
                            at[dim] = rest % 8
                            rest //= 8
                        else:
                            at[dim] = 7 if shift[dim] == 1 else 0
                    hi[r, q] = at[0] + 1
                    lo[r, q] = at[1] * 8 + at[2]
    return np.concatenate([hi, lo], axis=1)


def kernel(
    feat_hbm, occ, nbr, send, cot_hbm, w1_hbm, w2_hbm, qtab_hbm, ptab_hbm, otab_hbm,
    out,
    feat, cot, qtab, ptab, w1, w2, nbrv, occb, sel, oh, um, uh, ug, hsend, own, win_m, win_h, tm, th, gpad, pre, grads,
    psend, precv, asend, arecv, zsend, zrecv, lrecv, bsend, brecv, gath,
    wsem, hs, hr, ps, pr, as_, ar, zs, zr, gs, gr, osem, bs, br,
):
    d = lax.axis_index("dp")
    s = lax.axis_index("space")
    core = lax.rem(d, 2)
    y = d // 2
    x = lax.rem(s, NX)
    z = s // NX
    not_core = 1 - core
    pa = x * not_core + y * core
    pb = y * not_core + x * core

    near_x = [x] + [lax.rem(x + j, NX) for j in range(1, NX)]
    near_y = [y] + [lax.rem(y + j, NY) for j in range(1, NY)]
    near_z = [z] + [lax.rem(z + j, NZ) for j in range(1, NZ)]
    near_a = [i * not_core + j * core for i, j in zip(near_x, near_y)]
    near_b = [j * not_core + i * core for i, j in zip(near_x, near_y)]
    row_y = [2 * j + core for j in near_y]
    ring_dev = [(d * not_core + row_y[j] * core, z * NX + (near_x[j] * not_core + x * core)) for j in range(4)]
    b_dp = [row_y[j] * not_core + d * core for j in range(4)]
    b_sp = [x * not_core + near_x[j] * core for j in range(4)]
    row_z = [j * NX for j in near_z]

    def plane_dev(j):
        return (b_dp[j % 4], row_z[j // 4] + b_sp[j % 4])

    def group_dev(dy, dc):
        return (2 * near_y[dy] + (not_core if dc else core), s)

    relations = [(dy, dc) for dy in range(NY) for dc in range(2) if dy or dc]

    loads = []
    for n, (src, dst) in enumerate(
        ((ptab_hbm, ptab), (feat_hbm, feat), (qtab_hbm, qtab), (otab_hbm, oh.at[:, pl.ds(0, OWN)]), (w1_hbm, w1), (cot_hbm, cot), (w2_hbm, w2))
    ):
        loads.append(pltpu.make_async_copy(src, dst, wsem.at[n]))
        loads[-1].start()

    barrier = pltpu.get_barrier_semaphore()
    partners = [group_dev(dy, dc) for dy, dc in relations]
    partners += [ring_dev[j] for j in (1, 2, 3)]
    partners += [plane_dev(j) for j in range(1, 32)]
    partners += [(d, lax.rem(s + t + BRICKS, BRICKS)) for t in DISTANCES]
    for partner in partners:
        pl.semaphore_signal(barrier, inc=1, device_id=partner, device_id_type=MESH)

    pending = []

    def push(src, dst, send_sem, recv_sem, dev):
        copy = pltpu.make_async_remote_copy(
            src_ref=src, dst_ref=dst, send_sem=send_sem, recv_sem=recv_sem,
            device_id=dev, device_id_type=MESH,
        )
        copy.start()
        pending.append(copy)
        return copy

    occ_row = jnp.broadcast_to(occ[...].astype(F32), (LANES, VOX))
    for j in range(VOX // LANES):
        occb[pl.ds(j * LANES, LANES), :] = occ_row[:, j * LANES : (j + 1) * LANES].T

    def occupied():
        return jnp.concatenate([occb[...], occb[...]], axis=1)

    loads[1].wait()
    um[pl.ds(0, OWN), :] = (feat[...].astype(F32) * occupied()).astype(BF16)

    nbrv[...] = jnp.full((1, 128), -1, jnp.int32)
    nbrv[:, 0:26] = nbr[...]
    slots = nbrv[...]
    scale = jnp.where(lax.broadcasted_iota(jnp.int32, (256, 128), 0) < 128, 64.0, 1.0).astype(BF16)
    lane = lax.broadcasted_iota(jnp.int32, (PAY, 128), 1)
    loads[0].wait()
    for t in range(6):
        flag = send[0, t].astype(F32)
        chosen = jnp.where(slots == t, flag, 0.0)
        rows = ptab[...] * jnp.concatenate([chosen, chosen], axis=1)
        voxel = jnp.dot(rows.astype(BF16), scale, preferred_element_type=F32).astype(jnp.int32)
        for j in range(VOX // LANES):
            hit = voxel == lane + (64 + j * LANES)
            sel[pl.ds(t * PAY, PAY), pl.ds(j * LANES, LANES)] = jnp.where(hit, 1.0, 0.0).astype(BF16)

    pl.semaphore_wait(barrier, len(partners))

    def send_halo(which, field):
        packed = jnp.dot(sel[...], field[pl.ds(0, OWN), :], preferred_element_type=F32)
        hsend[which] = packed.astype(BF16)
        return [
            push(
                hsend.at[which, pl.ds(t * PAY, PAY)],
                field.at[pl.ds(OWN + (5 - t) * PAY, PAY)],
                hs.at[which, t],
                hr.at[which, 5 - t],
                (d, lax.rem(s + DISTANCES[t] + BRICKS, BRICKS)),
            )
            for t in range(6)
        ]

    sent = send_halo(0, um)

    distance = jnp.where(slots < 3, slots - 3, slots - 2)
    other = s + distance
    present = (slots >= 0) & (slots < 6) & (other >= 0) & (other < BRICKS)
    base = jnp.where(present, 64 * (8 + slots), 64 * 32).astype(F32)
    lane1 = lax.broadcasted_iota(jnp.int32, (1, 128), 1)
    base = jnp.where(lane1 < 26, base, jnp.where(lane1 == 26, 1.0, jnp.where(lane1 == 27, 64.0, 0.0)))
    ones = jnp.ones((128, 128), BF16)

    def lay(i, carry):
        at = pl.multiple_of(i * 80, 16)
        rows = qtab[pl.ds(at, 80), :].astype(F32) * base
        source = jnp.dot(rows.astype(BF16), ones, preferred_element_type=F32).astype(jnp.int32)
        lanes80 = lax.broadcasted_iota(jnp.int32, (80, 128), 1)
        for j in range(OWN // LANES, ROWS // LANES):
            hit = source == lanes80 + j * LANES
            oh[pl.ds(at, 80), pl.ds(j * LANES, LANES)] = jnp.where(hit, 1.0, 0.0).astype(BF16)
        return carry

    loads[2].wait()
    lax.fori_loop(0, 30, lay, 0, unroll=2)
    loads[3].wait()

    def lay_own(field):
        def one(i, carry):
            at = pl.ds(pl.multiple_of(i * 400, 16), 400)
            rows = oh[at, pl.ds(0, OWN)]
            own[at, :] = jnp.dot(rows, field[pl.ds(0, OWN), :], preferred_element_type=F32).astype(BF16)
            return carry

        lax.fori_loop(0, 6, one, 0)

    def build_windows(field, win):
        def one(oc, carry):
            for half in range(2):
                at = pl.ds(pl.multiple_of(oc * 800 + half * 400, 16), 400)
                rows = oh[at, pl.ds(OWN, 6 * PAY)]
                halo = jnp.dot(rows, field[pl.ds(OWN, 6 * PAY), :], preferred_element_type=F32)
                padded = (halo + own[at, :].astype(F32)).reshape(5, 80, C)
                for ob in range(3):
                    part = padded[:, ob * 8 : ob * 8 + 64].reshape(320, C).astype(BF16)
                    lanes = pl.ds(pl.multiple_of((ob * 3 + oc) * C, C), C)
                    win[pl.ds(half * 320, 320), lanes] = part
            return carry

        lax.fori_loop(0, 3, one, 0)

    def conv(win, weight):
        for m in range(2):
            acc = jnp.zeros((256, C), F32)
            for oa in range(3):
                acc = acc + jnp.dot(
                    win[pl.ds(oa * 64 + m * 256, 256), :],
                    weight[pl.ds(oa * 9 * C, 9 * C), :],
                    preferred_element_type=F32,
                )
            yield m, acc

    def slope(value):
        sig = jax.nn.sigmoid(value)
        return sig * (1.0 + value * (1.0 - sig))

    def half_occ(m):
        part = occb[pl.ds(m * 256, 256), :]
        return jnp.concatenate([part, part], axis=1)

    def transpose_windows(win, turned):
        def one(j, carry):
            at = pl.ds(pl.multiple_of(j * C, C), C)
            turned[at, :] = win[:, at].T
            return carry

        lax.fori_loop(0, 9, one, 0)

    gpad[pl.ds(0, 64), :] = jnp.zeros((64, C), BF16)
    gpad[pl.ds(576, 64), :] = jnp.zeros((64, C), BF16)

    lay_own(um)
    for copy in sent:
        copy.wait_recv()
    build_windows(um, win_m)
    loads[4].wait()
    for m, acc in conv(win_m, w1):
        value = acc * half_occ(m)
        pre[pl.ds(m * 256, 256), :] = value
        uh[pl.ds(m * 256, 256), :] = (value * jax.nn.sigmoid(value)).astype(BF16)
    sent = send_halo(1, uh)
    lay_own(uh)
    transpose_windows(win_m, tm)
    for copy in sent:
        copy.wait_recv()
    build_windows(uh, win_h)
    loads[5].wait()
    loads[6].wait()
    for m, acc in conv(win_h, w2):
        rows = pl.ds(m * 256, 256)
        value = acc * half_occ(m) + um[rows, :].astype(F32)
        grad = (cot[rows, :].astype(F32) * slope(value) * half_occ(m)).astype(BF16)
        ug[rows, :] = grad
        gpad[pl.ds(64 + m * 256, 256), :] = grad
    sent = send_halo(2, ug)
    transpose_windows(win_h, th)

    def weight_grad(unit, turned):
        k7 = unit % 7
        for ky in range(4):
            k = ky * 7 + k7
            if k < 27:
                rows = pl.ds((k % 9) * C, C)
                if k // 9 == 1:
                    left, right = turned[rows, :], gpad[...]
                else:
                    left, right = turned[rows, pl.ds((k // 9) * 64, VOX)], gpad[pl.ds(64, VOX), :]
                res = jnp.dot(left, right, preferred_element_type=F32).reshape(NZ, NX, 8, C)
            else:
                res = jnp.zeros((NZ, NX, 8, C), F32)
            for xx in range(NX):
                grads[0, xx, :, pl.ds(unit_row(unit, ky), 8), :] = res[:, xx, :, :LANES]
                grads[1, ky, :, pl.ds(unit_row(unit, xx), 8), :] = res[:, xx, :, LANES:]

    def unit_row(unit, b):
        lo, n = next(f for f in FLOWS if f[0] <= unit < f[0] + f[1])
        return lo * 32 + b * n * 8 + (unit - lo) * 8

    def pair_start(f):
        lo, n = FLOWS[f]
        part = pl.ds(lo * 32, n * 32)
        copies = []
        for j in range(4):
            block = near_b[(j + 1) % 4]

            def cast(i, carry):
                psend[block, i, part, :] = grads[not_core, block, i, part, :].astype(BF16)
                return carry

            lax.fori_loop(0, NZ, cast, 0, unroll=UNROLL)
            copies.append(
                push(
                    psend.at[block, :, part],
                    precv.at[block, :, part],
                    ps.at[f, j],
                    pr.at[f, j],
                    (d + not_core - core, s),
                )
            )
        return copies

    def ring_start(f, pairs):
        lo, n = FLOWS[f]
        part = pl.ds(lo * 32, n * 32)
        copies = []
        for j in range(4):
            block = near_a[(j + 1) % 4]
            pairs[j].wait_recv()

            def add(i, carry):
                total = grads[core, block, i, part, :] + precv[block, i, part, :].astype(F32)
                if j < 3:
                    asend[j, i, part, :] = total.astype(BF16)
                else:
                    grads[core, pa, i, part, :] = total
                return carry

            lax.fori_loop(0, NZ, add, 0, unroll=UNROLL)
            if j < 3:
                copies.append(
                    push(asend.at[j, :, part], arecv.at[j, :, part], as_.at[f, j], ar.at[f, j], ring_dev[j + 1])
                )
        return copies

    def plane_copy(f, j):
        lo, n = FLOWS[f]
        rows = pl.ds(pl.multiple_of(lo * 32 + near_b[j % 4] * (n * 8), 16), n * 8)
        return pltpu.make_async_remote_copy(
            src_ref=zsend.at[near_z[j // 4], rows],
            dst_ref=zrecv.at[j, pl.ds(lo * 8, n * 8)],
            send_sem=zs.at[f],
            recv_sem=zr.at[f],
            device_id=plane_dev(j),
            device_id_type=MESH,
        )

    def plane_all(f, sem):
        lo, n = FLOWS[f]
        here = zrecv.at[pl.ds(1, 31), pl.ds(lo * 8, n * 8)]
        return pltpu.make_async_copy(here, here, sem.at[f])

    def line_copy(f, j):
        lo, n = FLOWS[f]
        part = pl.ds(lo * 32, n * 32)
        return pltpu.make_async_remote_copy(
            src_ref=zsend.at[near_z[j], part],
            dst_ref=lrecv.at[j, part],
            send_sem=zs.at[f],
            recv_sem=zr.at[f],
            device_id=plane_dev(4 * j),
            device_id_type=MESH,
        )

    def line_all(f, sem):
        lo, n = FLOWS[f]
        here = lrecv.at[pl.ds(1, 7), pl.ds(lo * 32, n * 32)]
        return pltpu.make_async_copy(here, here, sem.at[f])

    def across_start(f):
        lo, n = FLOWS[f]
        part = pl.ds(lo * 32, n * 32)
        line_all(f, zr).wait()
        total = grads[core, pa, z, part, :]
        for j in range(1, 8):
            total = total + lrecv[j, part, :].astype(F32)
        bsend[part, :] = total
        return [
            push(
                bsend.at[pl.ds(pl.multiple_of(lo * 32 + near_b[j] * (n * 8), 8), n * 8)],
                brecv.at[j, pl.ds(lo * 8, n * 8)],
                bs.at[f, j],
                br.at[f, j],
                plane_dev(j),
            )
            for j in range(1, 4)
        ]

    def plane_start(f, before):
        lo, n = FLOWS[f]
        part = pl.ds(lo * 32, n * 32)
        for copy in before:
            copy.wait_recv()

        def add(i, carry):
            far = arecv[0, i, part, :].astype(F32) + arecv[1, i, part, :].astype(F32)
            total = grads[core, pa, i, part, :] + (far + arecv[2, i, part, :].astype(F32))
            grads[core, pa, i, part, :] = total
            zsend[i, part, :] = total.astype(BF16)
            return carry

        lax.fori_loop(0, NZ, add, 0, unroll=UNROLL)

        if f < SPLIT:
            for j in (4, 3, 5, 2, 6, 1, 7):
                line_copy(f, j).start()
        else:
            for j in range(1, 32):
                plane_copy(f, j).start()

    def gather_start(f):
        lo, n = FLOWS[f]
        part = pl.ds(lo * 8, n * 8)
        mine = pl.ds(pl.multiple_of(lo * 32 + pb * (n * 8), 8), n * 8)

        if f < SPLIT:
            for copy in flow[f]:
                copy.wait_recv()
            total = bsend[mine, :]
            for j in range(1, 4):
                total = total + brecv[j, part, :]
        else:
            plane_all(f, zr).wait()
            total = grads[core, pa, z, mine, :]
            for j in range(1, 32):
                total = total + zrecv[j, part, :].astype(F32)
        gath[part, :] = total
        here = gath.at[part]
        there = out.at[y, core, part]
        kept = pltpu.make_async_copy(here, there, osem.at[f])
        kept.start()
        owned.append(kept)
        return [
            push(here, there, gs.at[f, n_], gr.at[f, n_], group_dev(dy, dc))
            for n_, (dy, dc) in enumerate(relations)
        ]

    flow = [None] * len(FLOWS)
    owned = []

    def pair(f):
        flow[f] = pair_start(f)

    def ring(f):
        flow[f] = ring_start(f, flow[f])

    def plane(f):
        plane_start(f, flow[f])
        flow[f] = []

    def across(f):
        flow[f] = across_start(f)

    def gather(f):
        flow[f] = gather_start(f)

    def units(f, which):
        lo, n = FLOWS[f]
        for unit in range(lo, lo + n):
            if unit // 7 == which:
                weight_grad(unit, (th, tm)[which])

    units(0, 0)
    pair(0)
    units(1, 0)
    ring(0)
    pair(1)
    units(2, 0)
    lay_own(ug)

    for copy in sent:
        copy.wait_recv()
    build_windows(ug, win_h)
    ring(1)
    for m in range(2):
        acc = jnp.zeros((256, C), F32)
        for oa in range(3):
            weights = jnp.concatenate([w2[pl.ds((26 - oa * 9 - j) * C, C), :] for j in range(9)], axis=1)
            acc = acc + lax.dot_general(
                win_h[pl.ds(oa * 64 + m * 256, 256), :],
                weights,
                (((1,), (1,)), ((), ())),
                preferred_element_type=F32,
            )
        rows = pl.ds(m * 256, 256)
        gpad[pl.ds(64 + m * 256, 256), :] = (acc * slope(pre[rows, :]) * half_occ(m)).astype(BF16)
    units(2, 1)
    pair(2)
    plane(0)
    units(3, 1)
    pair(3)
    ring(2)
    units(4, 1)
    pair(4)
    plane(1)
    ring(3)
    ring(4)
    across(0)
    plane(2)
    across(1)
    gather(0)
    plane(3)
    gather(1)
    plane(4)
    gather(2)
    gather(3)
    gather(4)
    for copies in flow:
        for copy in copies:
            copy.wait_recv()
    for kept in owned:
        kept.wait()
    for copy in pending:
        copy.wait_send()
    for f in range(len(FLOWS)):
        (line_all if f < SPLIT else plane_all)(f, zs).wait()


def local(features, occupancy, nbr_slots, send_mask, cotangent, weight_one, weight_two):
    vmem = pl.BlockSpec(memory_space=pltpu.VMEM)
    smem = pl.BlockSpec(memory_space=pltpu.SMEM)
    hbm = pl.BlockSpec(memory_space=pl.ANY)
    dma = pltpu.SemaphoreType.DMA
    res = pl.pallas_call(
        kernel,
        out_shape=jax.ShapeDtypeStruct((NY, 2, UNITS * 8, LANES), F32),
        in_specs=[hbm, vmem, vmem, smem, hbm, hbm, hbm, hbm, hbm, hbm],
        out_specs=hbm,
        scratch_shapes=[
            pltpu.VMEM((VOX, C), BF16),
            pltpu.VMEM((VOX, C), BF16),
            pltpu.VMEM((2400, 128), BF16),
            pltpu.VMEM((PAY, 256), F32),
            pltpu.VMEM((27 * C, C), BF16),
            pltpu.VMEM((27 * C, C), BF16),
            pltpu.VMEM((1, 128), jnp.int32),
            pltpu.VMEM((VOX, LANES), F32),
            pltpu.VMEM((6 * PAY, VOX), BF16),
            pltpu.VMEM((2400, ROWS), BF16),
            pltpu.VMEM((ROWS, C), BF16),
            pltpu.VMEM((ROWS, C), BF16),
            pltpu.VMEM((ROWS, C), BF16),
            pltpu.VMEM((3, 6 * PAY, C), BF16),
            pltpu.VMEM((2400, C), BF16),
            pltpu.VMEM((640, 9 * C), BF16),
            pltpu.VMEM((640, 9 * C), BF16),
            pltpu.VMEM((9 * C, 640), BF16),
            pltpu.VMEM((9 * C, 640), BF16),
            pltpu.VMEM((640, C), BF16),
            pltpu.VMEM((VOX, C), F32),
            pltpu.VMEM((2, 4, NZ, ROWS_ALL, LANES), F32),
            pltpu.VMEM((4, NZ, ROWS_ALL, LANES), BF16),
            pltpu.VMEM((4, NZ, ROWS_ALL, LANES), BF16),
            pltpu.VMEM((3, NZ, ROWS_ALL, LANES), BF16),
            pltpu.VMEM((3, NZ, ROWS_ALL, LANES), BF16),
            pltpu.VMEM((NZ, ROWS_ALL, LANES), BF16),
            pltpu.VMEM((32, UNITS * 8, LANES), BF16),
            pltpu.VMEM((8, ROWS_ALL, LANES), BF16),
            pltpu.VMEM((ROWS_ALL, LANES), F32),
            pltpu.VMEM((4, UNITS * 8, LANES), F32),
            pltpu.VMEM((UNITS * 8, LANES), F32),
            dma((7,)),
            dma((3, 6)),
            dma((3, 6)),
            dma((len(FLOWS), 4)),
            dma((len(FLOWS), 4)),
            dma((len(FLOWS), 3)),
            dma((len(FLOWS), 3)),
            dma((len(FLOWS),)),
            dma((len(FLOWS),)),
            dma((len(FLOWS), 7)),
            dma((len(FLOWS), 7)),
            dma((len(FLOWS),)),
            dma((len(FLOWS), 4)),
            dma((len(FLOWS), 4)),
        ],
        compiler_params=pltpu.CompilerParams(
            collective_id=0, has_side_effects=True, vmem_limit_bytes=60 * 1024 * 1024
        ),
    )(
        features.reshape(VOX, C),
        occupancy.reshape(1, VOX),
        nbr_slots.reshape(1, 26),
        send_mask.reshape(1, 6),
        cotangent.reshape(VOX, C),
        weight_one.reshape(27 * C, C),
        weight_two.reshape(27 * C, C),
        jnp.asarray(padded_table(), BF16),
        jnp.asarray(payload_table(), F32),
        jnp.asarray(own_table(), BF16),
    )
    res = res.reshape(NY, 2, 2, 7, 8, LANES).transpose(2, 4, 0, 3, 1, 5).reshape(2, 8, KP, C)[:, :, :27]
    return res[1], res[0]


def solution(mesh):
    in_specs = (
        P("dp", "space", None, None),
        P("dp", "space", None),
        P("dp", "space", None),
        P("dp", "space", None),
        P("dp", "space", None, None),
        P(),
        P(),
    )
    out_specs = (P("space", None, None), P("space", None, None))
    return jax.shard_map(local, mesh=mesh, in_specs=in_specs, out_specs=out_specs, check_vma=False)
```

```python
import jax
import jax.numpy as jnp
import numpy as np
from jax import lax
from jax.experimental import pallas as pl
from jax.experimental.pallas import tpu as pltpu
from jax.sharding import PartitionSpec as P

E = 8
VOX = E**3
C = 256
NX, NY, NZ = 4, 4, 8
BRICKS = NX * NZ
DISTANCES = (-3, -2, -1, 1, 2, 3)
PAY = E * E
OWN = VOX
ROWS = VOX + 6 * PAY
KP = 28
SPLIT = 2
UNITS = 14
UNROLL = 4
FLOWS = ((0, 2), (2, 4), (6, 4), (10, 2), (12, 2))
ROWS_ALL = UNITS * 4 * 8
LANES = 128
F32 = jnp.float32
BF16 = jnp.bfloat16
MESH = pl.DeviceIdType.MESH


def offset_index(shift):
    number = (shift[0] + 1) * 9 + (shift[1] + 1) * 3 + (shift[2] + 1)
    return None if number == 13 else (number if number < 13 else number - 1)


def padded_table():
    table = np.zeros((3, 10, 10, 8, 128), np.float32)
    for oc in range(3):
        for a in range(10):
            for b in range(10):
                for c in range(8):
                    at = (a, b, c + oc)
                    shift = [-1 if t == 0 else (1 if t == 9 else 0) for t in at]
                    free = [t - 1 for t, m in zip(at, shift) if m == 0]
                    q = offset_index(shift)
                    line = table[oc, a, b, c]
                    if q is None:
                        line[27] = free[0]
                        line[26] = free[1] * 8 + free[2]
                    else:
                        line[q] = 1
                        row = 0
                        for t in free:
                            row = row * 8 + t
                        line[26] = row
    return table.reshape(3 * 800, 128)


def own_table():
    table = padded_table()
    own = ~(table[:, :26] != 0).any(axis=1)
    source = np.where(own, 64 * table[:, 27] + table[:, 26], -1)
    return (source[:, None] == np.arange(OWN)[None, :]).astype(np.float32)


def payload_table():
    hi = np.zeros((PAY, 128), np.float32)
    lo = np.zeros((PAY, 128), np.float32)
    for a in (-1, 0, 1):
        for b in (-1, 0, 1):
            for c in (-1, 0, 1):
                shift = (a, b, c)
                q = offset_index(shift)
                if q is None:
                    continue
                n_free = sum(t == 0 for t in shift)
                for r in range(8**n_free):
                    rest, at = r, [0, 0, 0]
                    for dim in (2, 1, 0):
                        if shift[dim] == 0:
                            at[dim] = rest % 8
                            rest //= 8
                        else:
                            at[dim] = 7 if shift[dim] == 1 else 0
                    hi[r, q] = at[0] + 1
                    lo[r, q] = at[1] * 8 + at[2]
    return np.concatenate([hi, lo], axis=1)


def kernel(
    feat_hbm, occ, nbr, send, cot_hbm, w1_hbm, w2_hbm, qtab_hbm, ptab_hbm, otab_hbm,
    out,
    feat, cot, qtab, ptab, w1, w2, nbrv, occb, sel, oh, um, uh, ug, hsend, own, win_m, win_h, tm, th, gpad, pre, grads,
    psend, precv, asend, arecv, zsend, zrecv, lrecv, bsend, brecv, gath,
    wsem, hs, hr, ps, pr, as_, ar, zs, zr, gs, gr, osem, bs, br,
):
    d = lax.axis_index("dp")
    s = lax.axis_index("space")
    core = lax.rem(d, 2)
    y = d // 2
    x = lax.rem(s, NX)
    z = s // NX
    not_core = 1 - core
    pa = x * not_core + y * core
    pb = y * not_core + x * core

    near_x = [x] + [lax.rem(x + j, NX) for j in range(1, NX)]
    near_y = [y] + [lax.rem(y + j, NY) for j in range(1, NY)]
    near_z = [z] + [lax.rem(z + j, NZ) for j in range(1, NZ)]
    near_a = [i * not_core + j * core for i, j in zip(near_x, near_y)]
    near_b = [j * not_core + i * core for i, j in zip(near_x, near_y)]
    row_y = [2 * j + core for j in near_y]
    ring_dev = [(d * not_core + row_y[j] * core, z * NX + (near_x[j] * not_core + x * core)) for j in range(4)]
    b_dp = [row_y[j] * not_core + d * core for j in range(4)]
    b_sp = [x * not_core + near_x[j] * core for j in range(4)]
    row_z = [j * NX for j in near_z]

    def plane_dev(j):
        return (b_dp[j % 4], row_z[j // 4] + b_sp[j % 4])

    def group_dev(dy, dc):
        return (2 * near_y[dy] + (not_core if dc else core), s)

    relations = [(dy, dc) for dy in range(NY) for dc in range(2) if dy or dc]

    loads = []
    for n, (src, dst) in enumerate(
        ((ptab_hbm, ptab), (feat_hbm, feat), (qtab_hbm, qtab), (otab_hbm, oh.at[:, pl.ds(0, OWN)]), (w1_hbm, w1), (cot_hbm, cot), (w2_hbm, w2))
    ):
        loads.append(pltpu.make_async_copy(src, dst, wsem.at[n]))
        loads[-1].start()

    barrier = pltpu.get_barrier_semaphore()
    partners = [group_dev(dy, dc) for dy, dc in relations]
    partners += [ring_dev[j] for j in (1, 2, 3)]
    partners += [plane_dev(j) for j in range(1, 32)]
    partners += [(d, lax.rem(s + t + BRICKS, BRICKS)) for t in DISTANCES]
    for partner in partners:
        pl.semaphore_signal(barrier, inc=1, device_id=partner, device_id_type=MESH)

    pending = []

    def push(src, dst, send_sem, recv_sem, dev):
        copy = pltpu.make_async_remote_copy(
            src_ref=src, dst_ref=dst, send_sem=send_sem, recv_sem=recv_sem,
            device_id=dev, device_id_type=MESH,
        )
        copy.start()
        pending.append(copy)
        return copy

    occ_row = jnp.broadcast_to(occ[...].astype(F32), (LANES, VOX))
    for j in range(VOX // LANES):
        occb[pl.ds(j * LANES, LANES), :] = occ_row[:, j * LANES : (j + 1) * LANES].T

    def occupied():
        return jnp.concatenate([occb[...], occb[...]], axis=1)

    loads[1].wait()
    um[pl.ds(0, OWN), :] = (feat[...].astype(F32) * occupied()).astype(BF16)

    nbrv[...] = jnp.full((1, 128), -1, jnp.int32)
    nbrv[:, 0:26] = nbr[...]
    slots = nbrv[...]
    scale = jnp.where(lax.broadcasted_iota(jnp.int32, (256, 128), 0) < 128, 64.0, 1.0).astype(BF16)
    lane = lax.broadcasted_iota(jnp.int32, (PAY, 128), 1)
    loads[0].wait()
    for t in range(6):
        flag = send[0, t].astype(F32)
        chosen = jnp.where(slots == t, flag, 0.0)
        rows = ptab[...] * jnp.concatenate([chosen, chosen], axis=1)
        voxel = jnp.dot(rows.astype(BF16), scale, preferred_element_type=F32).astype(jnp.int32)
        for j in range(VOX // LANES):
            hit = voxel == lane + (64 + j * LANES)
            sel[pl.ds(t * PAY, PAY), pl.ds(j * LANES, LANES)] = jnp.where(hit, 1.0, 0.0).astype(BF16)

    pl.semaphore_wait(barrier, len(partners))

    def send_halo(which, field):
        packed = jnp.dot(sel[...], field[pl.ds(0, OWN), :], preferred_element_type=F32)
        hsend[which] = packed.astype(BF16)
        return [
            push(
                hsend.at[which, pl.ds(t * PAY, PAY)],
                field.at[pl.ds(OWN + (5 - t) * PAY, PAY)],
                hs.at[which, t],
                hr.at[which, 5 - t],
                (d, lax.rem(s + DISTANCES[t] + BRICKS, BRICKS)),
            )
            for t in range(6)
        ]

    sent = send_halo(0, um)

    distance = jnp.where(slots < 3, slots - 3, slots - 2)
    other = s + distance
    present = (slots >= 0) & (slots < 6) & (other >= 0) & (other < BRICKS)
    base = jnp.where(present, 64 * (8 + slots), 64 * 32).astype(F32)
    lane1 = lax.broadcasted_iota(jnp.int32, (1, 128), 1)
    base = jnp.where(lane1 < 26, base, jnp.where(lane1 == 26, 1.0, jnp.where(lane1 == 27, 64.0, 0.0)))
    ones = jnp.ones((128, 128), BF16)

    def lay(i, carry):
        at = pl.multiple_of(i * 80, 16)
        rows = qtab[pl.ds(at, 80), :].astype(F32) * base
        source = jnp.dot(rows.astype(BF16), ones, preferred_element_type=F32).astype(jnp.int32)
        lanes80 = lax.broadcasted_iota(jnp.int32, (80, 128), 1)
        for j in range(OWN // LANES, ROWS // LANES):
            hit = source == lanes80 + j * LANES
            oh[pl.ds(at, 80), pl.ds(j * LANES, LANES)] = jnp.where(hit, 1.0, 0.0).astype(BF16)
        return carry

    loads[2].wait()
    lax.fori_loop(0, 30, lay, 0, unroll=2)
    loads[3].wait()

    def lay_own(field):
        def one(i, carry):
            at = pl.ds(pl.multiple_of(i * 400, 16), 400)
            rows = oh[at, pl.ds(0, OWN)]
            own[at, :] = jnp.dot(rows, field[pl.ds(0, OWN), :], preferred_element_type=F32).astype(BF16)
            return carry

        lax.fori_loop(0, 6, one, 0, unroll=2)

    def build_windows(field, win):
        def one(oc, carry):
            for half in range(2):
                at = pl.ds(pl.multiple_of(oc * 800 + half * 400, 16), 400)
                rows = oh[at, pl.ds(OWN, 6 * PAY)]
                halo = jnp.dot(rows, field[pl.ds(OWN, 6 * PAY), :], preferred_element_type=F32)
                padded = (halo + own[at, :].astype(F32)).reshape(5, 80, C)
                for ob in range(3):
                    part = padded[:, ob * 8 : ob * 8 + 64].reshape(320, C).astype(BF16)
                    lanes = pl.ds(pl.multiple_of((ob * 3 + oc) * C, C), C)
                    win[pl.ds(half * 320, 320), lanes] = part
            return carry

        lax.fori_loop(0, 3, one, 0)

    def conv(win, weight):
        for m in range(2):
            acc = jnp.zeros((256, C), F32)
            for oa in range(3):
                acc = acc + jnp.dot(
                    win[pl.ds(oa * 64 + m * 256, 256), :],
                    weight[pl.ds(oa * 9 * C, 9 * C), :],
                    preferred_element_type=F32,
                )
            yield m, acc

    def slope(value):
        sig = jax.nn.sigmoid(value)
        return sig * (1.0 + value * (1.0 - sig))

    def half_occ(m):
        part = occb[pl.ds(m * 256, 256), :]
        return jnp.concatenate([part, part], axis=1)

    def transpose_windows(win, turned):
        def one(j, carry):
            at = pl.ds(pl.multiple_of(j * C, C), C)
            turned[at, :] = win[:, at].T
            return carry

        lax.fori_loop(0, 9, one, 0, unroll=3)

    gpad[pl.ds(0, 64), :] = jnp.zeros((64, C), BF16)
    gpad[pl.ds(576, 64), :] = jnp.zeros((64, C), BF16)

    lay_own(um)
    for copy in sent:
        copy.wait_recv()
    build_windows(um, win_m)
    loads[4].wait()
    for m, acc in conv(win_m, w1):
        value = acc * half_occ(m)
        pre[pl.ds(m * 256, 256), :] = value
        uh[pl.ds(m * 256, 256), :] = (value * jax.nn.sigmoid(value)).astype(BF16)
    sent = send_halo(1, uh)
    lay_own(uh)
    transpose_windows(win_m, tm)
    for copy in sent:
        copy.wait_recv()
    build_windows(uh, win_h)
    loads[5].wait()
    loads[6].wait()
    for m, acc in conv(win_h, w2):
        rows = pl.ds(m * 256, 256)
        value = acc * half_occ(m) + um[rows, :].astype(F32)
        grad = (cot[rows, :].astype(F32) * slope(value) * half_occ(m)).astype(BF16)
        ug[rows, :] = grad
        gpad[pl.ds(64 + m * 256, 256), :] = grad
    sent = send_halo(2, ug)
    transpose_windows(win_h, th)

    def weight_grad(unit, turned):
        k7 = unit % 7
        for ky in range(4):
            k = ky * 7 + k7
            if k < 27:
                rows = pl.ds((k % 9) * C, C)
                if k // 9 == 1:
                    left, right = turned[rows, :], gpad[...]
                else:
                    left, right = turned[rows, pl.ds((k // 9) * 64, VOX)], gpad[pl.ds(64, VOX), :]
                res = jnp.dot(left, right, preferred_element_type=F32).reshape(NZ, NX, 8, C)
            else:
                res = jnp.zeros((NZ, NX, 8, C), F32)
            for xx in range(NX):
                grads[0, xx, :, pl.ds(unit_row(unit, ky), 8), :] = res[:, xx, :, :LANES]
                grads[1, ky, :, pl.ds(unit_row(unit, xx), 8), :] = res[:, xx, :, LANES:]

    def unit_row(unit, b):
        lo, n = next(f for f in FLOWS if f[0] <= unit < f[0] + f[1])
        return lo * 32 + b * n * 8 + (unit - lo) * 8

    def pair_start(f):
        lo, n = FLOWS[f]
        part = pl.ds(lo * 32, n * 32)
        copies = []
        for j in range(4):
            block = near_b[(j + 1) % 4]

            def cast(i, carry):
                psend[block, i, part, :] = grads[not_core, block, i, part, :].astype(BF16)
                return carry

            lax.fori_loop(0, NZ, cast, 0, unroll=UNROLL)
            copies.append(
                push(
                    psend.at[block, :, part],
                    precv.at[block, :, part],
                    ps.at[f, j],
                    pr.at[f, j],
                    (d + not_core - core, s),
                )
            )
        return copies

    def ring_start(f, pairs):
        lo, n = FLOWS[f]
        part = pl.ds(lo * 32, n * 32)
        copies = []
        for j in range(4):
            block = near_a[(j + 1) % 4]
            pairs[j].wait_recv()

            def add(i, carry):
                total = grads[core, block, i, part, :] + precv[block, i, part, :].astype(F32)
                if j < 3:
                    asend[j, i, part, :] = total.astype(BF16)
                else:
                    grads[core, pa, i, part, :] = total
                return carry

            lax.fori_loop(0, NZ, add, 0, unroll=UNROLL)
            if j < 3:
                copies.append(
                    push(asend.at[j, :, part], arecv.at[j, :, part], as_.at[f, j], ar.at[f, j], ring_dev[j + 1])
                )
        return copies

    def plane_copy(f, j):
        lo, n = FLOWS[f]
        rows = pl.ds(pl.multiple_of(lo * 32 + near_b[j % 4] * (n * 8), 16), n * 8)
        return pltpu.make_async_remote_copy(
            src_ref=zsend.at[near_z[j // 4], rows],
            dst_ref=zrecv.at[j, pl.ds(lo * 8, n * 8)],
            send_sem=zs.at[f],
            recv_sem=zr.at[f],
            device_id=plane_dev(j),
            device_id_type=MESH,
        )

    def plane_all(f, sem):
        lo, n = FLOWS[f]
        here = zrecv.at[pl.ds(1, 31), pl.ds(lo * 8, n * 8)]
        return pltpu.make_async_copy(here, here, sem.at[f])

    def line_copy(f, j):
        lo, n = FLOWS[f]
        part = pl.ds(lo * 32, n * 32)
        return pltpu.make_async_remote_copy(
            src_ref=zsend.at[near_z[j], part],
            dst_ref=lrecv.at[j, part],
            send_sem=zs.at[f],
            recv_sem=zr.at[f],
            device_id=plane_dev(4 * j),
            device_id_type=MESH,
        )

    def line_all(f, sem):
        lo, n = FLOWS[f]
        here = lrecv.at[pl.ds(1, 7), pl.ds(lo * 32, n * 32)]
        return pltpu.make_async_copy(here, here, sem.at[f])

    def across_start(f):
        lo, n = FLOWS[f]
        part = pl.ds(lo * 32, n * 32)
        line_all(f, zr).wait()
        total = grads[core, pa, z, part, :]
        for j in range(1, 8):
            total = total + lrecv[j, part, :].astype(F32)
        bsend[part, :] = total
        return [
            push(
                bsend.at[pl.ds(pl.multiple_of(lo * 32 + near_b[j] * (n * 8), 8), n * 8)],
                brecv.at[j, pl.ds(lo * 8, n * 8)],
                bs.at[f, j],
                br.at[f, j],
                plane_dev(j),
            )
            for j in range(1, 4)
        ]

    def plane_start(f, before):
        lo, n = FLOWS[f]
        part = pl.ds(lo * 32, n * 32)
        for copy in before:
            copy.wait_recv()

        def add(i, carry):
            far = arecv[0, i, part, :].astype(F32) + arecv[1, i, part, :].astype(F32)
            total = grads[core, pa, i, part, :] + (far + arecv[2, i, part, :].astype(F32))
            grads[core, pa, i, part, :] = total
            zsend[i, part, :] = total.astype(BF16)
            return carry

        lax.fori_loop(0, NZ, add, 0, unroll=UNROLL)

        if f < SPLIT:
            for j in (4, 3, 5, 2, 6, 1, 7):
                line_copy(f, j).start()
        else:
            for j in range(1, 32):
                plane_copy(f, j).start()

    def gather_start(f):
        lo, n = FLOWS[f]
        part = pl.ds(lo * 8, n * 8)
        mine = pl.ds(pl.multiple_of(lo * 32 + pb * (n * 8), 8), n * 8)

        if f < SPLIT:
            for copy in flow[f]:
                copy.wait_recv()
            total = bsend[mine, :]
            for j in range(1, 4):
                total = total + brecv[j, part, :]
        else:
            plane_all(f, zr).wait()
            total = grads[core, pa, z, mine, :]
            for j in range(1, 32):
                total = total + zrecv[j, part, :].astype(F32)
        gath[part, :] = total
        here = gath.at[part]
        there = out.at[y, core, part]
        kept = pltpu.make_async_copy(here, there, osem.at[f])
        kept.start()
        owned.append(kept)
        return [
            push(here, there, gs.at[f, n_], gr.at[f, n_], group_dev(dy, dc))
            for n_, (dy, dc) in enumerate(relations)
        ]

    flow = [None] * len(FLOWS)
    owned = []

    def pair(f):
        flow[f] = pair_start(f)

    def ring(f):
        flow[f] = ring_start(f, flow[f])

    def plane(f):
        plane_start(f, flow[f])
        flow[f] = []

    def across(f):
        flow[f] = across_start(f)

    def gather(f):
        flow[f] = gather_start(f)

    def units(f, which):
        lo, n = FLOWS[f]
        for unit in range(lo, lo + n):
            if unit // 7 == which:
                weight_grad(unit, (th, tm)[which])

    units(0, 0)
    pair(0)
    units(1, 0)
    ring(0)
    pair(1)
    units(2, 0)
    lay_own(ug)

    for copy in sent:
        copy.wait_recv()
    build_windows(ug, win_h)
    ring(1)
    for m in range(2):
        acc = jnp.zeros((256, C), F32)
        for oa in range(3):
            weights = jnp.concatenate([w2[pl.ds((26 - oa * 9 - j) * C, C), :] for j in range(9)], axis=1)
            acc = acc + lax.dot_general(
                win_h[pl.ds(oa * 64 + m * 256, 256), :],
                weights,
                (((1,), (1,)), ((), ())),
                preferred_element_type=F32,
            )
        rows = pl.ds(m * 256, 256)
        gpad[pl.ds(64 + m * 256, 256), :] = (acc * slope(pre[rows, :]) * half_occ(m)).astype(BF16)
    units(2, 1)
    pair(2)
    plane(0)
    units(3, 1)
    pair(3)
    ring(2)
    units(4, 1)
    pair(4)
    plane(1)
    ring(3)
    ring(4)
    across(0)
    plane(2)
    across(1)
    gather(0)
    plane(3)
    gather(1)
    plane(4)
    gather(2)
    gather(3)
    gather(4)
    for copies in flow:
        for copy in copies:
            copy.wait_recv()
    for kept in owned:
        kept.wait()
    for copy in pending:
        copy.wait_send()
    for f in range(len(FLOWS)):
        (line_all if f < SPLIT else plane_all)(f, zs).wait()


def local(features, occupancy, nbr_slots, send_mask, cotangent, weight_one, weight_two):
    vmem = pl.BlockSpec(memory_space=pltpu.VMEM)
    smem = pl.BlockSpec(memory_space=pltpu.SMEM)
    hbm = pl.BlockSpec(memory_space=pl.ANY)
    dma = pltpu.SemaphoreType.DMA
    res = pl.pallas_call(
        kernel,
        out_shape=jax.ShapeDtypeStruct((NY, 2, UNITS * 8, LANES), F32),
        in_specs=[hbm, vmem, vmem, smem, hbm, hbm, hbm, hbm, hbm, hbm],
        out_specs=hbm,
        scratch_shapes=[
            pltpu.VMEM((VOX, C), BF16),
            pltpu.VMEM((VOX, C), BF16),
            pltpu.VMEM((2400, 128), BF16),
            pltpu.VMEM((PAY, 256), F32),
            pltpu.VMEM((27 * C, C), BF16),
            pltpu.VMEM((27 * C, C), BF16),
            pltpu.VMEM((1, 128), jnp.int32),
            pltpu.VMEM((VOX, LANES), F32),
            pltpu.VMEM((6 * PAY, VOX), BF16),
            pltpu.VMEM((2400, ROWS), BF16),
            pltpu.VMEM((ROWS, C), BF16),
            pltpu.VMEM((ROWS, C), BF16),
            pltpu.VMEM((ROWS, C), BF16),
            pltpu.VMEM((3, 6 * PAY, C), BF16),
            pltpu.VMEM((2400, C), BF16),
            pltpu.VMEM((640, 9 * C), BF16),
            pltpu.VMEM((640, 9 * C), BF16),
            pltpu.VMEM((9 * C, 640), BF16),
            pltpu.VMEM((9 * C, 640), BF16),
            pltpu.VMEM((640, C), BF16),
            pltpu.VMEM((VOX, C), F32),
            pltpu.VMEM((2, 4, NZ, ROWS_ALL, LANES), F32),
            pltpu.VMEM((4, NZ, ROWS_ALL, LANES), BF16),
            pltpu.VMEM((4, NZ, ROWS_ALL, LANES), BF16),
            pltpu.VMEM((3, NZ, ROWS_ALL, LANES), BF16),
            pltpu.VMEM((3, NZ, ROWS_ALL, LANES), BF16),
            pltpu.VMEM((NZ, ROWS_ALL, LANES), BF16),
            pltpu.VMEM((32, UNITS * 8, LANES), BF16),
            pltpu.VMEM((8, ROWS_ALL, LANES), BF16),
            pltpu.VMEM((ROWS_ALL, LANES), F32),
            pltpu.VMEM((4, UNITS * 8, LANES), F32),
            pltpu.VMEM((UNITS * 8, LANES), F32),
            dma((7,)),
            dma((3, 6)),
            dma((3, 6)),
            dma((len(FLOWS), 4)),
            dma((len(FLOWS), 4)),
            dma((len(FLOWS), 3)),
            dma((len(FLOWS), 3)),
            dma((len(FLOWS),)),
            dma((len(FLOWS),)),
            dma((len(FLOWS), 7)),
            dma((len(FLOWS), 7)),
            dma((len(FLOWS),)),
            dma((len(FLOWS), 4)),
            dma((len(FLOWS), 4)),
        ],
        compiler_params=pltpu.CompilerParams(
            collective_id=0, has_side_effects=True, vmem_limit_bytes=60 * 1024 * 1024
        ),
    )(
        features.reshape(VOX, C),
        occupancy.reshape(1, VOX),
        nbr_slots.reshape(1, 26),
        send_mask.reshape(1, 6),
        cotangent.reshape(VOX, C),
        weight_one.reshape(27 * C, C),
        weight_two.reshape(27 * C, C),
        jnp.asarray(padded_table(), BF16),
        jnp.asarray(payload_table(), F32),
        jnp.asarray(own_table(), BF16),
    )
    res = res.reshape(NY, 2, 2, 7, 8, LANES).transpose(2, 4, 0, 3, 1, 5).reshape(2, 8, KP, C)[:, :, :27]
    return res[1], res[0]


def solution(mesh):
    in_specs = (
        P("dp", "space", None, None),
        P("dp", "space", None),
        P("dp", "space", None),
        P("dp", "space", None),
        P("dp", "space", None, None),
        P(),
        P(),
    )
    out_specs = (P("space", None, None), P("space", None, None))
    return jax.shard_map(local, mesh=mesh, in_specs=in_specs, out_specs=out_specs, check_vma=False)
```
